32 devices in a mesh: tm: 2 (over core), gx: 4 (over y, x), gy: 4 (over z).
Axes of the slice: x: 2, y: 2, z: 4, core: 2. Of those that a mesh axis runs over, the one named last changes fastest.
Arguments:
- start_states: float32 [2, 128, 64, 256], P('tm', 'gx', 'gy'), may hold values from 0.5 to 2
- wind_code: int32 [4, 4], P('gx', 'gy'), may hold values from 0 to 7
- wind_profile: float32 [2, 256], replicated, may hold values from 0.05 to 0.4
- vertical_mix: float32 [128, 64, 256], P('gx', 'gy'), may hold values from 0.01 to 0.1
Outputs:
- middle_states: float32 [2, 128, 64, 256], P('tm', 'gx', 'gy')
- final_states: float32 [2, 128, 64, 256], P('tm', 'gx', 'gy')
The draws below stay inside these ranges and needn't reach their ends.
Inputs may be any that keep to these rules, and one draw needn't show every extreme that they name: `wind_code`: a regime code.
All inputs are finite; a program needn't handle non-finite values.
Results may differ from the reference program's by a relative error of at most 0.00002.
Values sent between devices are 32-bit elements; how exact they have to be, the bound alone decides.
No kernel may reach another device: no remote copies, remote signals or barrier semaphores. Data moves between devices by JAX's collectives and lax.ppermute only.
A program may use at most 64 MiB of HBM per device.

```python
import math
import jax
import jax.numpy as jnp
from jax import lax

BX = 32
BY = 16
NZ = 256
SWEEPS = 3
NX = 128
NY = 64
SLICES = 2


def touch_ends(drawn, own_key, least, high):
    longest = drawn.shape.index(max(drawn.shape))
    spots = []
    for shift in (0, 1):
        where = [jax.random.randint(jax.random.fold_in(own_key, axis), (), 0, length) for axis, length in enumerate(drawn.shape)]
        where[longest] = (where[longest] + shift) % drawn.shape[longest]
        spots.append(tuple(where))
    return drawn.at[spots[0]].set(least).at[spots[1]].set(high)


def steps_of(own_key, dims, split, low, high):
    factor_of, own = 1.0, jax.random.fold_in(own_key, 6)
    for axis_at, parts in split:
        steps = jnp.exp(jax.random.uniform(jax.random.fold_in(own, axis_at), (parts,), jnp.float32, low / len(split), high / len(split)))
        factor_of = factor_of * jnp.repeat(steps, dims[axis_at] // parts).reshape([-1 if axis == axis_at else 1 for axis in range(len(dims))])
    return factor_of


def setup_inputs(seed: int = 0) -> dict:
    splits = jax.random.split(jax.random.key(seed), 5)
    start_states = jnp.clip(0.5 + 1.5 * jax.random.uniform(splits[0], (SLICES, NX, NY, NZ), jnp.float32) ** steps_of(splits[0], (SLICES, NX, NY, NZ), ((0, 2), (1, 4), (2, 4)), -0.2, 0.2), 0.5, 2.0)
    wind_code = touch_ends(jax.random.randint(splits[1], (NX // BX, NY // BY), 0, 8), jax.random.fold_in(splits[1], 1), 0, 7).astype(jnp.int32)
    wind_profile = jnp.clip(jnp.exp(jax.random.uniform(splits[2], (2, NZ), jnp.float32, math.log(0.05), math.log(0.4))), 0.05, 0.4)
    vertical_mix = jnp.clip(jnp.exp(math.log(0.1) - 2.3025851 * jax.random.uniform(splits[3], (NX, NY, NZ), jnp.float32) ** steps_of(splits[3], (NX, NY, NZ), ((0, 4), (1, 4)), -0.2, 0.2)), 0.01, 0.1)
    return {"start_states": start_states, "wind_code": wind_code, "wind_profile": wind_profile, "vertical_mix": vertical_mix}


time_step = 0.5
half_step = 0.25
diffusion_low = 0.04
diffusion_high = 0.1
first_weights = (5.0 / 24.0, 1.0 / 3.0, -1.0 / 24.0)
second_weights = (-1.0 / 24.0, 1.0 / 3.0, 5.0 / 24.0)


def tendency(padded, sign_x, sign_y, strength, wind_profile, vertical_mix):
    row_count = padded.shape[0] - 4
    columns = padded.shape[1] - 4

    def neighbour(source, step_x, step_y):
        return source[2 + step_x:2 + step_x + row_count, 2 + step_y:2 + step_y + columns]

    centre = neighbour(padded, 0, 0)
    squared = padded * padded
    growth = squared / (1.0 + squared)
    growth_centre = neighbour(growth, 0, 0)
    spread = jnp.zeros_like(centre)
    for step_x, step_y in ((1, 0), (-1, 0), (0, 1), (0, -1)):
        weight = 0.5 + 0.5 * (growth_centre + neighbour(growth, step_x, step_y))
        spread = spread + weight * (neighbour(padded, step_x, step_y) - centre)
    upwind_x = jnp.where(sign_x > 0, neighbour(padded, -1, 0), neighbour(padded, 1, 0))
    farther_x = jnp.where(sign_x > 0, neighbour(padded, -2, 0), neighbour(padded, 2, 0))
    upwind_y = jnp.where(sign_y > 0, neighbour(padded, 0, -1), neighbour(padded, 0, 1))
    farther_y = jnp.where(sign_y > 0, neighbour(padded, 0, -2), neighbour(padded, 0, 2))
    carried = wind_profile[0] * (3.0 * centre - 4.0 * upwind_x + farther_x)
    carried = carried + wind_profile[1] * (3.0 * centre - 4.0 * upwind_y + farther_y)
    below_cells = jnp.concatenate([centre[:, :, :1], centre[:, :, :-1]], axis=2)
    above_cells = jnp.concatenate([centre[:, :, 1:], centre[:, :, -1:]], axis=2)
    return strength * spread - 0.5 * carried + vertical_mix * (below_cells + above_cells - 2.0 * centre)


def sweep_once(first_state, first_rate, slopes, tendency_of):
    middle = first_state + half_step * (first_rate - slopes[0]) + time_step * (
        first_weights[0] * slopes[0] + first_weights[1] * slopes[1] + first_weights[2] * slopes[2])
    middle_rate = tendency_of(middle)
    final_state = middle + half_step * (middle_rate - slopes[1]) + time_step * (
        second_weights[0] * slopes[0] + second_weights[1] * slopes[1] + second_weights[2] * slopes[2])
    final_rate = tendency_of(final_state)
    return (first_state, middle, final_state), (first_rate, middle_rate, final_rate)


def reference(start_states, wind_code, wind_profile, vertical_mix):
    regime = jnp.repeat(jnp.repeat(wind_code, BX, axis=0), BY, axis=1)[:, :, None]
    sign_x = 1.0 - 2.0 * (regime % 2).astype(jnp.float32)
    sign_y = 1.0 - 2.0 * ((regime // 2) % 2).astype(jnp.float32)
    strength = jnp.where(regime // 4 == 1, diffusion_high, diffusion_low)

    def tendency_of(state_field):
        padded = jnp.pad(state_field, ((2, 2), (2, 2), (0, 0)))
        return tendency(padded, sign_x, sign_y, strength, wind_profile, vertical_mix)

    def slice_step(previous, initial_state):
        initial_rate = tendency_of(initial_state)
        states = (initial_state, initial_state, initial_state)
        slopes = (initial_rate, initial_rate, initial_rate)
        finals = [initial_state]
        for sweep_index in range(SWEEPS):
            first_state = previous[sweep_index]
            first_rate = tendency_of(first_state)
            states, slopes = sweep_once(first_state, first_rate, slopes, tendency_of)
            finals.append(states[2])
        return jnp.stack(finals[:SWEEPS]), (states[1], states[2])

    carried_ends = jnp.broadcast_to(start_states[0], (SWEEPS,) + start_states.shape[1:])
    unused, outputs = lax.scan(slice_step, carried_ends, start_states)
    return outputs[0], outputs[1]
```

```python
import functools
import jax
import jax.numpy as jnp
from jax import lax
from jax.experimental import pallas as pl
from jax.experimental.pallas import tpu as pltpu
from jax.sharding import PartitionSpec as P

SWEEPS = 3
HALO = 4 * SWEEPS
LANES = 128
TILE = 8
time_step = 0.5
half_step = 0.25
diffusion_low = 0.04
diffusion_high = 0.1
first_weights = (5.0 / 24.0, 1.0 / 3.0, -1.0 / 24.0)
second_weights = (-1.0 / 24.0, 1.0 / 3.0, 5.0 / 24.0)


def row_classes(reach, own):
    steps = reach // 2
    groups = {}
    for a in range(steps, -1, -1):
        beside = 2 * (steps - a) if a else reach
        tiles = -(-(own + 2 * beside) // TILE)
        groups.setdefault(tiles, []).append(a)
    out = []
    for tiles, members in sorted(groups.items()):
        beside = max(2 * (steps - a) if a else reach for a in members)
        out.append((tiles, HALO - beside, min(members), max(members)))
    return out


def growth(u):
    return 0.75 - 0.5 / (1.0 + u * u)


def sweeps(n, slices, own_rows, own_columns, codes, wind, mix, first, g0, g1, mid, act, middle_out, final_out):
    halves = mix.shape[0]
    lane = lax.broadcasted_iota(jnp.int32, (TILE, LANES), 1)
    line = lax.broadcasted_iota(jnp.int32, (TILE, LANES), 0)
    bottom, top = lane == 0, lane == LANES - 1
    cx = [jnp.broadcast_to(-0.5 * wind[0:1, z * LANES:(z + 1) * LANES], (TILE, LANES)) for z in range(halves)]
    cy = [jnp.broadcast_to(-0.5 * wind[1:2, z * LANES:(z + 1) * LANES], (TILE, LANES)) for z in range(halves)]
    c3 = [3.0 * (a + b) for a, b in zip(cx, cy)]
    parity = lax.rem(n, 2)
    before = jnp.maximum(n - 1, 0)
    other = lax.rem(before, 2)
    fslot = jnp.where(n == 0, 0, 1 + parity)

    def prior(sweep):
        if sweep == 1:
            return before, jnp.where(before == 0, 0, 1 + other)
        return (jnp.where(n == 0, 0, slices + 2 * other + sweep - 2),
                jnp.where(n == 0, 0, 3 + 2 * other + sweep - 2))

    def evaluate(reach, source, active, finish):
        def block(x, column, tiles):
            for k in range(tiles):
                y = column + TILE * k
                edges = [e for e in (HALO, HALO + own_columns) if y < e < y + TILE]
                sides = [sum(p >= e for e in (HALO, HALO + own_columns)) for p in [y] + edges]
                words = [codes[x * 3 + j] for j in sides]
                kh = [jnp.where(w >= 8, 0.0, jnp.where(w >= 4, diffusion_high, diffusion_low)) for w in words]
                step_x = [1 - 2 * lax.rem(w, 2) for w in words]
                step_y = [1 - 2 * lax.rem(w // 2, 2) for w in words]

                def merge(parts):
                    got = parts[-1]
                    for e, part in zip(reversed(edges), reversed(parts[:-1])):
                        got = jnp.where(line < e - y, part, got)
                    return got
                strength = merge([jnp.full((TILE, LANES), s, jnp.float32) for s in kh])
                u = [{} for _ in range(halves)]
                for z in range(halves):
                    src, a_ref = source(z), active(z)
                    col = {i: src[x + i, pl.ds(y, TILE), :] for i in (-1, 0, 1, 2)}
                    act_c = {i: a_ref[x + i, pl.ds(y, TILE), :] for i in (-1, 0, 1, 2)}
                    flux = [(act_c[i] + act_c[i + 1]) * (col[i + 1] - col[i]) for i in (-1, 0, 1)]
                    for r in range(2):
                        uc, ac = col[r], act_c[r]
                        spread = flux[r + 1] - flux[r]
                        for s in (1, -1):
                            un = src[x + r, pl.ds(y + s, TILE), :]
                            an = a_ref[x + r, pl.ds(y + s, TILE), :]
                            spread = spread + (ac + an) * (un - uc)
                        near_x = merge([src[x + r - s, pl.ds(y, TILE), :] for s in step_x])
                        far_x = merge([src[x + r - 2 * s, pl.ds(y, TILE), :] for s in step_x])
                        near_y = merge([src[x + r, pl.ds(y - s, TILE), :] for s in step_y])
                        far_y = merge([src[x + r, pl.ds(y - 2 * s, TILE), :] for s in step_y])
                        total = (strength * spread + c3[z] * uc + cx[z] * (far_x - 4.0 * near_x)
                                 + cy[z] * (far_y - 4.0 * near_y))
                        u[z][r] = (uc, total)
                for r in range(2):
                    ups = [pltpu.roll(u[z][r][0], LANES - 1, 1) for z in range(halves)]
                    downs = [pltpu.roll(u[z][r][0], 1, 1) for z in range(halves)]
                    rates = []
                    for z in range(halves):
                        uc, total = u[z][r]
                        above = jnp.where(top, ups[z + 1] if z + 1 < halves else uc, ups[z])
                        below = jnp.where(bottom, downs[z - 1] if z else uc, downs[z])
                        rates.append(total + mix[z, x + r, pl.ds(y, TILE), :] * ((above - uc) + (below - uc)))
                    finish(x + r, y, rates, [u[z][r][0] for z in range(halves)])

        for tiles, column, near, far in row_classes(reach, own_columns):
            if near == 0:
                count, begin = own_rows // 2 + 2 * far, HALO - 2 * far

                @pl.loop(0, count)
                def _(i, begin=begin, column=column, tiles=tiles):
                    block(begin + 2 * i, column, tiles)
            else:
                width = far - near + 1

                @pl.loop(0, 2 * width)
                def _(i, column=column, tiles=tiles, near=near, far=far, width=width):
                    low = HALO - 2 * far + 2 * i
                    high = HALO + own_rows + 2 * (near - 1) + 2 * (i - width)
                    block(jnp.where(i < width, low, high), column, tiles)

    def at(ref, *lead):
        return lambda z: ref.at[(*lead, z)]

    def put(ref, lead, z, x, y, value):
        ref[(*lead, z, x, pl.ds(y, TILE), slice(None))] = value

    def get(ref, lead, z, x, y):
        return ref[(*lead, z, x, pl.ds(y, TILE), slice(None))]

    w1 = [time_step * w for w in first_weights]
    w2 = [time_step * w for w in second_weights]
    q1, q2 = sum(w1), sum(w2)
    first_1, g0_1 = prior(1)
    first_2, g0_2 = prior(2)
    first_3, g0_3 = prior(3)
    last_1, last_2 = slices + 2 * parity, slices + 2 * parity + 1
    rate_1, rate_2 = 3 + 2 * parity, 4 + 2 * parity
    start = n == 0

    def end_1(x, y, rates, us):
        for z, f in enumerate(rates):
            put(g0, (fslot,), z, x, y, f)
            g = jnp.where(start, f, get(g0, (g0_1,), z, x, y))
            m = get(first, (first_1,), z, x, y) + half_step * (g - f) + q1 * f
            put(mid, (), z, x, y, m)
            put(act, (1,), z, x, y, growth(m))

    def end_2(x, y, rates, us):
        for z, g in enumerate(rates):
            put(g1, (0,), z, x, y, g)
            f = get(g0, (fslot,), z, x, y)
            last = us[z] + half_step * (g - f) + q2 * f
            put(first, (last_1,), z, x, y, last)
            put(act, (0,), z, x, y, growth(last))

    def end_3(x, y, rates, us):
        for z, g in enumerate(rates):
            put(g0, (rate_1,), z, x, y, g)
            m = (get(first, (first_2,), z, x, y) + half_step * get(g0, (g0_2,), z, x, y)
                 + (w1[0] - half_step) * get(g0, (g0_1,), z, x, y) + w1[1] * get(g1, (0,), z, x, y) + w1[2] * g)
            put(mid, (), z, x, y, m)
            put(act, (1,), z, x, y, growth(m))

    def end_4(x, y, rates, us):
        for z, g in enumerate(rates):
            put(g1, (1,), z, x, y, g)
            last = (us[z] + half_step * g + w2[0] * get(g0, (g0_1,), z, x, y)
                    + (w2[1] - half_step) * get(g1, (0,), z, x, y) + w2[2] * get(g0, (rate_1,), z, x, y))
            put(first, (last_2,), z, x, y, last)
            put(act, (0,), z, x, y, growth(last))

    def end_5(x, y, rates, us):
        for z, g in enumerate(rates):
            put(g0, (rate_2,), z, x, y, g)
            m = (get(first, (first_3,), z, x, y) + half_step * get(g0, (g0_3,), z, x, y)
                 + (w1[0] - half_step) * get(g0, (g0_2,), z, x, y) + w1[1] * get(g1, (1,), z, x, y) + w1[2] * g)
            put(mid, (), z, x, y, m)
            put(act, (1,), z, x, y, growth(m))

    def end_6(x, y, rates, us):
        for z, g in enumerate(rates):
            last = (us[z] + half_step * g + w2[0] * get(g0, (g0_2,), z, x, y)
                    + (w2[1] - half_step) * get(g1, (1,), z, x, y) + w2[2] * get(g0, (rate_2,), z, x, y))
            where = (n, x - HALO, pl.ds(y - HALO, TILE), pl.ds(z * LANES, LANES))
            middle_out[where] = us[z]
            final_out[where] = last

    evaluate(10, at(first, n), at(act, 0), end_1)
    evaluate(8, at(mid), at(act, 1), end_2)
    evaluate(6, at(first, last_1), at(act, 0), end_3)
    evaluate(4, at(mid), at(act, 1), end_4)
    evaluate(2, at(first, last_2), at(act, 0), end_5)
    evaluate(0, at(mid), at(act, 1), end_6)


def outside(word, low_x, low_y):
    return jnp.where(word == 0, 8 + (0 if low_x else 1) + (0 if low_y else 2), word - 1)


def fill(first, act, mix, a, z, x, y, value, slices):
    where = (z, x, pl.ds(y, value.shape[0]), slice(None))
    if a < slices:
        first[(a, *where)] = value
    else:
        mix[where] = value


def corner_rows():
    offset = 0
    for d in range(HALO):
        wide = HALO - 2 * (d // 2 + 1)
        if wide:
            yield d, offset, wide
            offset += wide


CORNER = sum(w for _, _, w in corner_rows())


def pack_kernel(where_ref, code, own, other, mixing, beside_x, beside_y, diagonal_1, diagonal_2):
    t = where_ref[0]
    rows, columns, levels = own.shape
    halves = levels // LANES
    deep = rows - HALO
    word = jnp.full((TILE, LANES), (code[0, 0] + 1).astype(jnp.float32))
    beside_x[beside_x.shape[0] - 1] = jnp.full(beside_x.shape[1:], (code[0, 0] + 1).astype(jnp.float32))
    for ref in (beside_y, diagonal_1, diagonal_2):
        ref[0, 0, pl.ds(ref.shape[2] - TILE, TILE), :] = word

    def side(low):
        for a, pair in enumerate(((own, other) if low else (other, own), (other, own) if low else (own, other), None)):
            ref = mixing if pair is None else pair[0]
            if a < 2:
                ref = (own, other)[a] if low else (other, own)[a]
            at_x = 0 if low else deep
            beside_x[pl.ds(a * HALO, HALO)] = ref[pl.ds(at_x, HALO)]
            at_y = 0 if low else columns - HALO
            for z in range(halves):
                lanes = pl.ds(z * LANES, LANES)

                @pl.loop(0, rows)
                def _(x):
                    line = ref[x, :, lanes]
                    beside_y[a, z, pl.ds(x * HALO, HALO), :] = line[at_y:at_y + HALO]
                for d, offset, wide in corner_rows():
                    x = d if low else rows - 1 - d
                    line = ref[x, :, lanes]
                    near, far = line[:wide], line[columns - wide:]
                    diagonal_1[a, z, pl.ds(offset, wide), :] = near if low else far
                    diagonal_2[a, z, pl.ds(offset, wide), :] = far if low else near

    pl.when(t == 0)(lambda: side(True))
    pl.when(t != 0)(lambda: side(False))


def pair_kernel(where_ref, code, wind, own, other, mixing, halo_x, halo_y, passed_y, corner_1, corner_2,
                middle_out, final_out, first, g0, g1, mid, act, mix, codes):
    t = where_ref[0]
    block_rows, columns, levels = own.shape
    halves = levels // LANES
    half = block_rows // 2
    inner = half + HALO
    tail = halo_y.shape[2] - TILE

    def word_of(tile):
        return jnp.max(tile).astype(jnp.int32)

    word_x = word_of(halo_x[halo_x.shape[0] - 1, pl.ds(0, TILE), pl.ds(0, LANES)])
    word_y, word_p = word_of(halo_y[0, 0, pl.ds(tail, TILE), :]), word_of(passed_y[0, 0, pl.ds(tail, TILE), :])
    word_1 = word_of(corner_1[0, 0, pl.ds(corner_1.shape[2] - TILE, TILE), :])
    word_2 = word_of(corner_2[0, 0, pl.ds(corner_2.shape[2] - TILE, TILE), :])

    def side(low):
        at_own, from_own, at_x = (HALO, 0, 0) if low else (0, block_rows - inner, inner)
        low_y, high_y = (halo_y, passed_y) if low else (passed_y, halo_y)
        low_corner, high_corner = (corner_1, corner_2) if low else (corner_2, corner_1)
        word_low, word_high = (word_y, word_p) if low else (word_p, word_y)
        corner_low, corner_high = (word_1, word_2) if low else (word_2, word_1)

        @pl.loop(0, inner)
        def _(i):
            codes[(at_own + i) * 3] = outside(word_low, True, True)
            codes[(at_own + i) * 3 + 1] = code[0, 0]
            codes[(at_own + i) * 3 + 2] = outside(word_high, True, False)

        @pl.loop(0, HALO)
        def _(i):
            codes[(at_x + i) * 3] = outside(corner_low, low, True)
            codes[(at_x + i) * 3 + 1] = outside(word_x, low, True)
            codes[(at_x + i) * 3 + 2] = outside(corner_high, low, False)

        for a in range(3):
            ref = mixing if a == 2 else ((own, other)[a] if low else (other, own)[a])
            for z in range(halves):
                lanes = pl.ds(z * LANES, LANES)

                @pl.loop(0, inner)
                def _(i):
                    x = from_own + i
                    for y in range(0, columns, TILE):
                        fill(first, act, mix, a, z, at_own + i, HALO + y, ref[x, pl.ds(y, TILE), lanes], 2)
                    fill(first, act, mix, a, z, at_own + i, 0, low_y[a, z, pl.ds(x * HALO, HALO), :], 2)
                    fill(first, act, mix, a, z, at_own + i, HALO + columns, high_y[a, z, pl.ds(x * HALO, HALO), :], 2)

                @pl.loop(0, HALO)
                def _(i):
                    for y in range(0, columns, TILE):
                        fill(first, act, mix, a, z, at_x + i, HALO + y, halo_x[a * HALO + i, pl.ds(y, TILE), lanes], 2)
                for d, offset, wide in corner_rows():
                    x = HALO - 1 - d if low else inner + d
                    fill(first, act, mix, a, z, x, HALO - wide, low_corner[a, z, pl.ds(offset, wide), :], 2)
                    fill(first, act, mix, a, z, x, HALO + columns, high_corner[a, z, pl.ds(offset, wide), :], 2)

    pl.when(t == 0)(lambda: side(True))
    pl.when(t != 0)(lambda: side(False))

    @pl.loop(0, 2)
    def _(n):
        activate(n, first, act)
        sweeps(n, 2, half, columns, codes, wind, mix, first, g0, g1, mid, act, middle_out, final_out)


def activate(n, first, act):
    rows, columns = first.shape[2:4]

    @pl.loop(0, rows)
    def _(x):
        for z in range(first.shape[1]):
            for y in range(0, columns, TILE):
                act[0, z, x, pl.ds(y, TILE), :] = growth(first[n, z, x, pl.ds(y, TILE), :])


def planes(slices, rows, columns, levels):
    plane = (levels // LANES, rows, columns + TILE, LANES)
    return [pltpu.VMEM((k, *plane), jnp.float32) for k in (slices + 4, 7, 2)] + [
        pltpu.VMEM(plane, jnp.float32), pltpu.VMEM((2, *plane), jnp.float32), pltpu.VMEM(plane, jnp.float32)]


VMEM = pl.BlockSpec(memory_space=pltpu.VMEM)
SMEM = pl.BlockSpec(memory_space=pltpu.SMEM)
LIMIT = 56 * 2**20


def of(*shape):
    return jax.ShapeDtypeStruct(shape, jnp.float32)


def pair_solution(state, code, wind, mixing, sizes):
    axes = ("tm", "gx", "gy")
    rows, columns, levels = state.shape
    halves = levels // LANES
    t = lax.axis_index("tm")
    where = t.astype(jnp.int32).reshape(1)

    def partners(step_x, step_y):
        pairs = []
        for x in range(sizes[1]):
            for y in range(sizes[2]):
                u, v = x - step_x, y - step_y
                if 0 <= u < sizes[1] and 0 <= v < sizes[2]:
                    here, there = x * sizes[2] + y, (sizes[1] + u) * sizes[2] + v
                    pairs += [(here, there), (there, here)]
        return pairs

    swap = [(0, 1), (1, 0)]
    other = lax.ppermute(state, "tm", swap)
    packed = pl.pallas_call(
        pack_kernel,
        out_shape=(of(3 * HALO + 1, columns, levels), of(3, halves, rows * HALO + TILE, LANES),
                   of(3, halves, CORNER + 12, LANES), of(3, halves, CORNER + 12, LANES)),
        in_specs=[SMEM, SMEM, VMEM, VMEM, VMEM], out_specs=[VMEM] * 4,
        compiler_params=pltpu.CompilerParams(vmem_limit_bytes=LIMIT),
    )(where, code, state, other, mixing)
    halo_x = lax.ppermute(packed[0], axes, partners(1, 0))
    halo_y = lax.ppermute(packed[1], axes, partners(0, 1))
    corner_1 = lax.ppermute(packed[2], axes, partners(1, 1))
    corner_2 = lax.ppermute(packed[3], axes, partners(1, -1))
    passed_y = lax.ppermute(halo_y, "tm", swap)
    half = rows // 2
    out = of(2, half, columns, levels)
    middle, final = pl.pallas_call(
        pair_kernel, out_shape=(out, out),
        in_specs=[SMEM, SMEM] + [VMEM] * 9, out_specs=[VMEM] * 2,
        scratch_shapes=planes(2, half + 2 * HALO, columns + 2 * HALO, levels) + [
            pltpu.SMEM((3 * (half + 2 * HALO),), jnp.int32)],
        compiler_params=pltpu.CompilerParams(vmem_limit_bytes=LIMIT),
    )(where, code, wind, state, other, mixing, halo_x, halo_y, passed_y, corner_1, corner_2)
    both = jnp.stack([middle, final])
    mine = lax.dynamic_index_in_dim(both, t, 1, keepdims=False)
    got = lax.ppermute(lax.dynamic_index_in_dim(both, 1 - t, 1, keepdims=False), "tm", swap)
    whole = jnp.where(t == 0, jnp.concatenate([mine, got], 1), jnp.concatenate([got, mine], 1))
    return whole[0][None], whole[1][None]


def whole_kernel(own_rows, own_columns, codes, wind, state, mixing, middle_out, final_out, first, g0, g1, mid, act, mix):
    slices, rows, columns, levels = state.shape

    @pl.loop(0, rows)
    def _(x):
        for z in range(levels // LANES):
            lanes = pl.ds(z * LANES, LANES)
            for y in range(0, columns, TILE):
                mix[z, x, pl.ds(y, TILE), :] = mixing[x, pl.ds(y, TILE), lanes]
                for n in range(slices):
                    first[n, z, x, pl.ds(y, TILE), :] = state[n, x, pl.ds(y, TILE), lanes]

    @pl.loop(0, slices)
    def _(n):
        activate(n, first, act)
        sweeps(n, slices, own_rows, own_columns, codes, wind, mix, first, g0, g1, mid, act, middle_out, final_out)


def padded(x, sides, width):
    for axis, dim in sides:
        devices, length = lax.axis_size(axis), x.shape[dim]
        up = [(i, i + 1) for i in range(devices - 1)]
        down = [(j, i) for i, j in up]
        before = lax.ppermute(lax.slice_in_dim(x, length - width, length, axis=dim), axis, up)
        after = lax.ppermute(lax.slice_in_dim(x, 0, width, axis=dim), axis, down)
        x = jnp.concatenate([before, x, after], axis=dim)
    return x


def any_solution(state, code, wind, mixing, sizes):
    slices = sizes[0]
    rows, columns, levels = state.shape
    t, share = lax.axis_index("tm"), rows // slices
    wide = padded(jnp.stack([state, mixing]), (("gx", 1), ("gy", 2)), HALO)
    words = padded((code + 1).astype(jnp.float32), (("gx", 0), ("gy", 1)), 1).astype(jnp.int32)
    table = jnp.stack([jnp.stack([outside(words[i, j], i == 0, j == 0) for j in range(3)]) for i in range(3)])
    cut = functools.partial(lax.dynamic_slice_in_dim, start_index=t * share, slice_size=share + 2 * HALO)
    state = cut(lax.all_gather(wide[0], "tm"), axis=1)
    mixing = cut(wide[1], axis=0)
    line = t * share + jnp.arange(share + 2 * HALO)
    codes = table[(line >= HALO).astype(jnp.int32) + (line >= HALO + rows).astype(jnp.int32)].reshape(-1)
    out = of(slices, share, columns, levels)
    both = pl.pallas_call(
        functools.partial(whole_kernel, share, columns), out_shape=(out, out),
        in_specs=[SMEM] + [VMEM] * 3, out_specs=[VMEM] * 2,
        scratch_shapes=planes(slices, share + 2 * HALO, columns + 2 * HALO, levels),
        compiler_params=pltpu.CompilerParams(vmem_limit_bytes=LIMIT),
    )(codes, wind, state, mixing)
    return tuple(lax.all_to_all(x, "tm", 0, 1, tiled=True) for x in both)


def solution(mesh):
    sizes = tuple(mesh.shape[a] for a in ("tm", "gx", "gy"))
    run = pair_solution if sizes[0] == 2 else any_solution

    def shards(start_states, wind_code, wind_profile, vertical_mix):
        return run(start_states[0], wind_code, wind_profile, vertical_mix, sizes)

    in_specs = (P("tm", "gx", "gy", None), P("gx", "gy"), P(), P("gx", "gy", None))
    out_specs = (P("tm", "gx", "gy", None), P("tm", "gx", "gy", None))
    return jax.shard_map(shards, mesh=mesh, in_specs=in_specs, out_specs=out_specs, check_vma=False)
```

```python
import functools
import jax
import jax.numpy as jnp
from jax import lax
from jax.experimental import pallas as pl
from jax.experimental.pallas import tpu as pltpu
from jax.sharding import PartitionSpec as P

SWEEPS = 3
HALO = 4 * SWEEPS
LANES = 128
TILE = 8
time_step = 0.5
half_step = 0.25
diffusion_low = 0.04
diffusion_high = 0.1
first_weights = (5.0 / 24.0, 1.0 / 3.0, -1.0 / 24.0)
second_weights = (-1.0 / 24.0, 1.0 / 3.0, 5.0 / 24.0)


def row_classes(reach, own):
    steps = reach // 2
    groups = {}
    for a in range(steps + 1):
        beside = 2 * (steps - a) if a else reach
        groups.setdefault((-(-(own + 2 * beside) // TILE), a == 0), []).append((a, beside))
    out = []
    for (tiles, _), members in sorted(groups.items()):
        beside = max(b for _, b in members)
        begins = range(max(2, HALO + own + beside - TILE * tiles), HALO - beside + 1)
        cuts = lambda begin: sum(begin < e < begin + TILE * tiles and (e - begin) % TILE > 0 for e in (HALO, HALO + own))
        out.append((tiles, min(begins, key=cuts), members[0][0], members[-1][0]))
    return out


def growth(u):
    return 1.5 - 1.0 / (1.0 + u * u)


def sweeps(own_rows, own_columns, codes, wind, mix, start, mid, last_1, last_2, f, g1, g1b, g2, g2b, act_a, act_b,
           write):
    halves = mix.shape[0]
    slices, parts = range(start.shape[0]), range(halves)
    scale = 0.5 * half_step
    lane = lax.broadcasted_iota(jnp.int32, (TILE, LANES), 1)
    line = lax.broadcasted_iota(jnp.int32, (TILE, LANES), 0)
    bottom, top = lane == 0, lane == LANES - 1
    cx = [jnp.broadcast_to(-0.5 * half_step * wind[0:1, z * LANES:(z + 1) * LANES], (TILE, LANES)) for z in parts]
    cy = [jnp.broadcast_to(-0.5 * half_step * wind[1:2, z * LANES:(z + 1) * LANES], (TILE, LANES)) for z in parts]
    c3 = [3.0 * (a + b) for a, b in zip(cx, cy)]

    def merge(edges, values):
        got = values[-1]
        for e, value in zip(reversed(edges), reversed(values[:-1])):
            got = jnp.where(line < e, value, got)
        return got

    def evaluate(reach, source, active, finish):
        def block(x, count, column, tiles):
            rows = range(count)
            puts, below_flux = [], {}
            for k in range(tiles):
                y = column + TILE * k
                edges = [e - y for e in (HALO, HALO + own_columns) if y < e < y + TILE]
                sides = [sum(p >= e for e in (HALO, HALO + own_columns)) for p in [y] + [y + e for e in edges]]
                words = [codes[x * 3 + j] for j in sides]
                kh = [jnp.where(w >= 8, 0.0, jnp.where(w >= 4, scale * diffusion_high, scale * diffusion_low)) for w in words]
                step_x = [1 - 2 * (w & 1) for w in words]
                step_y = [1 - (w & 2) for w in words]
                strength = merge(edges, [jnp.full((TILE, LANES), s, jnp.float32) for s in kh])
                rates = {}
                for n in slices:
                    def u_at(z, i, j):
                        return source[n, z, x + i, pl.ds(y + j, TILE), :]

                    def a_at(z, i, j):
                        return active[n, z, x + i, pl.ds(y + j, TILE), :]

                    centre = {(z, r): u_at(z, r, 0) for z in parts for r in rows}
                    ups = {c: pltpu.roll(u, LANES - 1, 1) for c, u in centre.items()}
                    downs = {c: pltpu.roll(u, 1, 1) for c, u in centre.items()}
                    total = {}
                    for z in parts:
                        col = [u_at(z, -1, 0)] + [centre[z, r] for r in rows] + [u_at(z, count, 0)]
                        act = [a_at(z, i, 0) for i in range(-1, count + 1)]
                        flux = [(act[i] + act[i + 1]) * (col[i + 1] - col[i]) for i in range(count + 1)]
                        for r in rows:
                            uc, ac = col[r + 1], act[r + 1]
                            up = (ac + a_at(z, r, 1)) * (u_at(z, r, 1) - uc)
                            moved = pltpu.roll(up, 1, 0)
                            if k:
                                down = jnp.where(line == 0, below_flux[n, z, r], moved)
                            else:
                                down = (ac + a_at(z, r, -1)) * (uc - u_at(z, r, -1))
                            below_flux[n, z, r] = moved
                            spread = (flux[r + 1] - flux[r]) + (up - down)
                            near_x = merge(edges, [u_at(z, r - s, 0) for s in step_x])
                            far_x = merge(edges, [u_at(z, r - 2 * s, 0) for s in step_x])
                            near_y = merge(edges, [u_at(z, r, -s) for s in step_y])
                            far_y = merge(edges, [u_at(z, r, -2 * s) for s in step_y])
                            total[z, r] = ((strength * spread + c3[z] * uc) + cx[z] * (far_x - 4.0 * near_x)
                                           + cy[z] * (far_y - 4.0 * near_y))
                    for r in rows:
                        for z in parts:
                            u = centre[z, r]
                            above = jnp.where(top, ups[z + 1, r] if z + 1 < halves else u, ups[z, r])
                            below = jnp.where(bottom, downs[z - 1, r] if z else u, downs[z, r])
                            bend = (above - u) + (below - u)
                            rate = total[z, r] + mix[z, x + r, pl.ds(y, TILE), :] * bend
                            rates[n, z, r] = rate

                            def get(ref, m=n):
                                return ref[m, z, x + r, pl.ds(y, TILE), :]

                            def put(ref, value):
                                puts.append((ref, (n, z, x + r, y), value))
                            finish(get, put, n, rates.get((n - 1, z, r), rate), u, rate)
            for ref, at, value in puts:
                write(ref, at, value)

        for tiles, column, near, far in row_classes(reach, own_columns):
            if near == 0:
                group = 4 if own_rows % 4 == 0 else 2

                @pl.loop(0, own_rows // group)
                def _(i, column=column, tiles=tiles, group=group):
                    block(HALO + group * i, group, column, tiles)
            else:
                span = 2 * (far - near + 1)
                group = 4 if span % 4 == 0 else 2
                width = span // group

                @pl.loop(0, 2 * width, unroll=2 if group == 2 else 1)
                def _(i, column=column, tiles=tiles, near=near, far=far, width=width, group=group):
                    low = HALO - 2 * far + group * i
                    high = HALO + own_rows + 2 * (near - 1) + group * (i - width)
                    block(jnp.where(i < width, low, high), group, column, tiles)

    w1 = [time_step / half_step * w for w in first_weights]
    w2 = [time_step / half_step * w for w in second_weights]
    assert abs(sum(w1) - 1) < 1e-12 and abs(sum(w2) - 1) < 1e-12

    def end_1(get, put, n, earlier, u, rate):
        m = get(start, max(n - 1, 0)) + ((earlier - rate) + rate)
        put(f, rate)
        put(mid, m)
        put(act_b, growth(m))

    def end_2(get, put, n, earlier, u, rate):
        first = get(f)
        last = u + ((rate - first) + first)
        put(g1, rate)
        put(last_1, last)
        put(act_a, growth(last))

    def end_3(get, put, n, earlier, u, rate):
        begin = get(last_1, n - 1) if n else get(start, 0)
        g0 = earlier if n else get(f, 0)
        m = begin + g0 + (w1[0] - 1.0) * get(f, max(n - 1, 0)) + w1[1] * get(g1) + w1[2] * rate
        put(g2, rate)
        put(mid, m)
        put(act_b, growth(m))

    def end_4(get, put, n, earlier, u, rate):
        last = u + rate + w2[0] * get(f, max(n - 1, 0)) + (w2[1] - 1.0) * get(g1) + w2[2] * get(g2)
        put(g1b, rate)
        put(last_2, last)
        put(act_a, growth(last))

    def end_5(get, put, n, earlier, u, rate):
        begin = get(last_2, n - 1) if n else get(start, 0)
        g0 = earlier if n else get(f, 0)
        before = get(g2, n - 1) if n else get(f, 0)
        m = begin + g0 + (w1[0] - 1.0) * before + w1[1] * get(g1b) + w1[2] * rate
        put(g2b, rate)
        put(mid, m)
        put(act_b, growth(m))

    def end_6(get, put, n, earlier, u, rate):
        before = get(g2, n - 1) if n else get(f, 0)
        put("middle", u)
        put("final", u + rate + w2[0] * before + (w2[1] - 1.0) * get(g1b) + w2[2] * get(g2b))

    evaluate(10, start, act_a, end_1)
    evaluate(8, mid, act_b, end_2)
    evaluate(6, last_1, act_a, end_3)
    evaluate(4, mid, act_b, end_4)
    evaluate(2, last_2, act_a, end_5)
    evaluate(0, mid, act_b, end_6)


def outside(word, low_x, low_y):
    return jnp.where(word == 0, 8 + (0 if low_x else 1) + (0 if low_y else 2), word - 1)


DEPTHS = (HALO, HALO, HALO - 2)


def corner_rows():
    out, offset = [], 0
    for a, depth in enumerate(DEPTHS):
        for d in range(depth - 2):
            wide = depth - 2 * (d // 2 + 1)
            out.append((a, d, offset, wide))
            offset += wide
    return out, offset


CORNER_ROWS, CORNER_SIZE = corner_rows()
BEFORE = tuple(sum(DEPTHS[:a]) for a in range(len(DEPTHS) + 1))


def pack_kernel(where_ref, code, own, other, mixing, beside_x, beside_y, diagonal_1, diagonal_2):
    t = where_ref[0]
    rows, columns, levels = own.shape
    word = jnp.full((TILE, LANES), (code[0, 0] + 1).astype(jnp.float32))
    for ref in (beside_x, beside_y, diagonal_1, diagonal_2):
        ref[0, pl.ds(ref.shape[1] - TILE, TILE), :] = word

    def side(low):
        arrays = (own, other, mixing) if low else (other, own, mixing)
        for z in range(levels // LANES):
            lanes = pl.ds(z * LANES, LANES)
            for a, depth in enumerate(DEPTHS):
                for i in range(depth):
                    x = i if low else rows - depth + i
                    beside_x[z, pl.ds((BEFORE[a] + i) * columns, columns), :] = arrays[a][x, :, lanes]
            for a, d, offset, wide in CORNER_ROWS:
                x = d if low else rows - 1 - d
                near, far = arrays[a][x, pl.ds(0, wide), lanes], arrays[a][x, pl.ds(columns - wide, wide), lanes]
                diagonal_1[z, pl.ds(offset, wide), :] = near if low else far
                diagonal_2[z, pl.ds(offset, wide), :] = far if low else near

        @pl.loop(0, rows // 2)
        def _(i):
            for x in (2 * i, 2 * i + 1):
                for z in range(levels // LANES):
                    for a, depth in enumerate(DEPTHS):
                        line = arrays[a][x, pl.ds(0 if low else columns - depth, depth), pl.ds(z * LANES, LANES)]
                        beside_y[z, pl.ds(BEFORE[a] * rows + x * depth, depth), :] = line

    pl.when(t == 0)(lambda: side(True))
    pl.when(t != 0)(lambda: side(False))


def pair_kernel(where_ref, code, wind, own, other, mixing, halo_x, halo_y, passed_y, corner_1, corner_2,
                mine_middle, mine_final, theirs, start, mid, last_1, last_2, f, g1, g1b, g2, g2b, act_a, act_b,
                mix, both, codes):
    t = where_ref[0]
    block_rows, columns, levels = own.shape
    halves = levels // LANES
    half = block_rows // 2
    inner = half + HALO

    def word_of(ref):
        return jnp.max(ref[0, pl.ds(ref.shape[1] - TILE, TILE), :]).astype(jnp.int32)

    word_x, word_y, word_p, word_1, word_2 = [word_of(r) for r in (halo_x, halo_y, passed_y, corner_1, corner_2)]

    def fill(a, z, x, y, value):
        at = (z, x, pl.ds(y, value.shape[0]), slice(None))
        if a < 2:
            start[(a, *at)] = value
            act_a[(a, *at)] = growth(value)
        else:
            mix[at] = half_step * value

    def side(low):
        at_own, from_own, at_x = (HALO, 0, 0) if low else (0, block_rows - inner, inner)
        low_y, high_y = (halo_y, passed_y) if low else (passed_y, halo_y)
        low_corner, high_corner = (corner_1, corner_2) if low else (corner_2, corner_1)
        word_low, word_high = (word_y, word_p) if low else (word_p, word_y)
        corner_low, corner_high = (word_1, word_2) if low else (word_2, word_1)
        arrays = (own, other, mixing) if low else (other, own, mixing)

        @pl.loop(0, inner)
        def _(i):
            codes[(at_own + i) * 3] = outside(word_low, True, True)
            codes[(at_own + i) * 3 + 1] = code[0, 0]
            codes[(at_own + i) * 3 + 2] = outside(word_high, True, False)

        @pl.loop(0, HALO)
        def _(i):
            codes[(at_x + i) * 3] = outside(corner_low, low, True)
            codes[(at_x + i) * 3 + 1] = outside(word_x, low, True)
            codes[(at_x + i) * 3 + 2] = outside(corner_high, low, False)

        @pl.loop(0, inner // 2)
        def _(pair):
            for i in (2 * pair, 2 * pair + 1):
                x = from_own + i
                for z in range(halves):
                    for a, depth in enumerate(DEPTHS):
                        for y in range(0, columns, TILE):
                            fill(a, z, at_own + i, HALO + y, arrays[a][x, pl.ds(y, TILE), pl.ds(z * LANES, LANES)])
                        at = pl.ds(BEFORE[a] * block_rows + x * depth, depth)
                        fill(a, z, at_own + i, HALO - depth, low_y[z, at, :])
                        fill(a, z, at_own + i, HALO + columns, high_y[z, at, :])

        for z in range(halves):
            for a, depth in enumerate(DEPTHS):
                for i in range(depth):
                    x = HALO - depth + i if low else inner + i
                    for y in range(0, columns, TILE):
                        fill(a, z, x, HALO + y, halo_x[z, pl.ds((BEFORE[a] + i) * columns + y, TILE), :])
            for a, d, offset, wide in CORNER_ROWS:
                x = HALO - 1 - d if low else inner + d
                fill(a, z, x, HALO - wide, low_corner[z, pl.ds(offset, wide), :])
                fill(a, z, x, HALO + columns, high_corner[z, pl.ds(offset, wide), :])

    pl.when(t == 0)(lambda: side(True))
    pl.when(t != 0)(lambda: side(False))

    def write(ref, at, value):
        n, z, x, y = at
        if isinstance(ref, str):
            place = jnp.where(t == n, 0, 1)
            both[place, 0 if ref == "middle" else 1, x - HALO, pl.ds(y - HALO, TILE), pl.ds(z * LANES, LANES)] = value
        else:
            ref[n, z, x, pl.ds(y, TILE), :] = value

    sweeps(half, columns, codes, wind, mix, start, mid, last_1, last_2, f, g1, g1b, g2, g2b, act_a, act_b, write)
    here = pl.ds(t * half, half)
    mine_middle[here] = both[0, 0]
    mine_final[here] = both[0, 1]
    theirs[...] = both[1]


VMEM = pl.BlockSpec(memory_space=pltpu.VMEM)
SMEM = pl.BlockSpec(memory_space=pltpu.SMEM)
LIMIT = 56 * 2**20


def of(*shape):
    return jax.ShapeDtypeStruct(shape, jnp.float32)


def pair_shards(state, code, wind, mixing, sizes):
    axes = ("tm", "gx", "gy")
    rows, columns, levels = state.shape
    halves = levels // LANES
    t = lax.axis_index("tm")
    where = t.astype(jnp.int32).reshape(1)

    def partners(step_x, step_y):
        pairs = []
        for x in range(sizes[1]):
            for y in range(sizes[2]):
                u, v = x - step_x, y - step_y
                if 0 <= u < sizes[1] and 0 <= v < sizes[2]:
                    here, there = x * sizes[2] + y, (sizes[1] + u) * sizes[2] + v
                    pairs += [(here, there), (there, here)]
        return pairs

    swap = [(0, 1), (1, 0)]
    other = lax.ppermute(state, "tm", swap)
    corner = of(halves, CORNER_SIZE + TILE, LANES)
    to_x, to_y, to_1, to_2 = pl.pallas_call(
        pack_kernel,
        out_shape=(of(halves, BEFORE[-1] * columns + TILE, LANES), of(halves, BEFORE[-1] * rows + TILE, LANES), corner, corner),
        in_specs=[SMEM, SMEM, VMEM, VMEM, VMEM], out_specs=[VMEM] * 4,
        compiler_params=pltpu.CompilerParams(vmem_limit_bytes=LIMIT),
    )(where, code, state, other, mixing)
    halo_x = lax.ppermute(to_x, axes, partners(1, 0))
    halo_y = lax.ppermute(to_y, axes, partners(0, 1))
    corner_1 = lax.ppermute(to_1, axes, partners(1, 1))
    corner_2 = lax.ppermute(to_2, axes, partners(1, -1))
    halo_x, halo_y, corner_1, corner_2 = lax.optimization_barrier((halo_x, halo_y, corner_1, corner_2))
    passed_y = lax.ppermute(halo_y, "tm", swap)
    half = rows // 2
    plane = (halves, half + 2 * HALO, columns + 2 * HALO + TILE, LANES)
    middle, final, theirs = pl.pallas_call(
        pair_kernel, out_shape=(of(*state.shape), of(*state.shape), of(2, half, columns, levels)),
        in_specs=[SMEM, SMEM] + [VMEM] * 9, out_specs=[VMEM] * 3,
        scratch_shapes=[pltpu.VMEM((2, *plane), jnp.float32)] * 11 + [
            pltpu.VMEM(plane, jnp.float32), pltpu.VMEM((2, 2, half, columns, levels), jnp.float32),
            pltpu.SMEM((3 * (half + 2 * HALO),), jnp.int32)],
        compiler_params=pltpu.CompilerParams(vmem_limit_bytes=LIMIT),
    )(where, code, wind, state, other, mixing, halo_x, halo_y, passed_y, corner_1, corner_2)
    got = lax.ppermute(theirs, "tm", swap)
    there = ((1 - t) * half, 0, 0)
    return lax.dynamic_update_slice(middle, got[0], there)[None], lax.dynamic_update_slice(final, got[1], there)[None]


def padded(x, sides, width):
    for axis, dim in sides:
        devices, length = lax.axis_size(axis), x.shape[dim]
        up = [(i, i + 1) for i in range(devices - 1)]
        down = [(j, i) for i, j in up]
        before = lax.ppermute(lax.slice_in_dim(x, length - width, length, axis=dim), axis, up)
        after = lax.ppermute(lax.slice_in_dim(x, 0, width, axis=dim), axis, down)
        x = jnp.concatenate([before, x, after], axis=dim)
    return x


def tendency(u, sign_x, sign_y, strength, wind, mixing):
    rows, columns = mixing.shape[:2]

    def beside(source, step_x, step_y):
        return source[2 + step_x:2 + step_x + rows, 2 + step_y:2 + step_y + columns]

    centre = beside(u, 0, 0)
    act = 0.5 * growth(u)
    spread = sum((beside(act, 0, 0) + beside(act, *s)) * (beside(u, *s) - centre) for s in ((1, 0), (-1, 0), (0, 1), (0, -1)))
    near_x, far_x = (jnp.where(sign_x > 0, beside(u, -k, 0), beside(u, k, 0)) for k in (1, 2))
    near_y, far_y = (jnp.where(sign_y > 0, beside(u, 0, -k), beside(u, 0, k)) for k in (1, 2))
    carried = wind[0] * (3.0 * centre - 4.0 * near_x + far_x) + wind[1] * (3.0 * centre - 4.0 * near_y + far_y)
    below = jnp.concatenate([centre[:, :, :1], centre[:, :, :-1]], axis=2)
    above = jnp.concatenate([centre[:, :, 1:], centre[:, :, -1:]], axis=2)
    return strength * spread - 0.5 * carried + mixing * (below + above - 2.0 * centre)


def slice_shards(state, code, wind, mixing, sizes):
    word = code[0, 0]
    strength = jnp.where(word // 4 == 1, diffusion_high, diffusion_low)

    def rate_of(u):
        return tendency(padded(u, (("gx", 0), ("gy", 1)), 2), 1 - 2 * (word % 2), 1 - 2 * (word // 2 % 2), strength, wind, mixing)

    start_rate = rate_of(state)
    last, rates = state, (start_rate,) * 3
    for _ in range(SWEEPS):
        arrived = lax.ppermute((last, rates[2]), "tm", [(i, i + 1) for i in range(sizes[0] - 1)])
        first, g0 = (jnp.where(lax.axis_index("tm") == 0, a, b) for a, b in zip((state, start_rate), arrived))
        middle = first + half_step * (g0 - rates[0]) + time_step * sum(w * r for w, r in zip(first_weights, rates))
        g1 = rate_of(middle)
        last = middle + half_step * (g1 - rates[1]) + time_step * sum(w * r for w, r in zip(second_weights, rates))
        rates = g0, g1, rate_of(last)
    return middle[None], last[None]


def solution(mesh):
    sizes = tuple(mesh.shape[a] for a in ("tm", "gx", "gy"))
    run = pair_shards if sizes[0] == 2 else slice_shards

    def shards(start_states, wind_code, wind_profile, vertical_mix):
        return run(start_states[0], wind_code, wind_profile, vertical_mix, sizes)

    in_specs = (P("tm", "gx", "gy", None), P("gx", "gy"), P(), P("gx", "gy", None))
    out_specs = (P("tm", "gx", "gy", None), P("tm", "gx", "gy", None))
    return jax.shard_map(shards, mesh=mesh, in_specs=in_specs, out_specs=out_specs, check_vma=False)
```

```python
import functools
import jax
import jax.numpy as jnp
from jax import lax
from jax.experimental import pallas as pl
from jax.experimental.pallas import tpu as pltpu
from jax.sharding import PartitionSpec as P

SWEEPS = 3
HALO = 4 * SWEEPS
LANES = 128
TILE = 8
time_step = 0.5
half_step = 0.25
diffusion_low = 0.04
diffusion_high = 0.1
first_weights = (5.0 / 24.0, 1.0 / 3.0, -1.0 / 24.0)
second_weights = (-1.0 / 24.0, 1.0 / 3.0, 5.0 / 24.0)


def row_classes(reach, own):
    steps = reach // 2
    groups = {}
    for a in range(steps + 1):
        beside = 2 * (steps - a) if a else reach
        groups.setdefault((-(-(own + 2 * beside) // TILE), a == 0), []).append((a, beside))
    out = []
    for (tiles, _), members in sorted(groups.items()):
        beside = max(b for _, b in members)
        begins = range(max(2, HALO + own + beside - TILE * tiles), HALO - beside + 1)
        cuts = lambda begin: sum(begin < e < begin + TILE * tiles and (e - begin) % TILE > 0 for e in (HALO, HALO + own))
        out.append((tiles, min(begins, key=cuts), members[0][0], members[-1][0]))
    return out


def growth(u):
    return 1.5 - 1.0 / (1.0 + u * u)


def sweeps(own_rows, own_columns, codes, wind, mix, start, mid, last_1, last_2, f, g1, g1b, g2, g2b, act_a, act_b,
           write):
    halves = mix.shape[0]
    slices, parts = range(start.shape[0]), range(halves)
    scale = 0.5 * half_step
    lane = lax.broadcasted_iota(jnp.int32, (TILE, LANES), 1)
    line = lax.broadcasted_iota(jnp.int32, (TILE, LANES), 0)
    bottom, top = lane == 0, lane == LANES - 1
    cx = [jnp.broadcast_to(-0.5 * half_step * wind[0:1, z * LANES:(z + 1) * LANES], (TILE, LANES)) for z in parts]
    cy = [jnp.broadcast_to(-0.5 * half_step * wind[1:2, z * LANES:(z + 1) * LANES], (TILE, LANES)) for z in parts]
    c3 = [3.0 * (a + b) for a, b in zip(cx, cy)]

    def merge(edges, values):
        got = values[-1]
        for e, value in zip(reversed(edges), reversed(values[:-1])):
            got = jnp.where(line < e, value, got)
        return got

    def evaluate(reach, source, active, finish):
        def block(x, count, column, tiles):
            rows = range(count)
            puts, below_flux = [], {}
            for k in range(tiles):
                y = column + TILE * k
                edges = [e - y for e in (HALO, HALO + own_columns) if y < e < y + TILE]
                sides = [sum(p >= e for e in (HALO, HALO + own_columns)) for p in [y] + [y + e for e in edges]]
                words = [codes[x * 3 + j] for j in sides]
                kh = [jnp.where(w >= 8, 0.0, jnp.where(w >= 4, scale * diffusion_high, scale * diffusion_low)) for w in words]
                step_x = [1 - 2 * (w & 1) for w in words]
                step_y = [1 - (w & 2) for w in words]
                strength = merge(edges, [jnp.full((TILE, LANES), s, jnp.float32) for s in kh])
                rates = {}
                for n in slices:
                    def u_at(z, i, j):
                        return source[n, z, x + i, pl.ds(y + j, TILE), :]

                    def a_at(z, i, j):
                        return active[n, z, x + i, pl.ds(y + j, TILE), :]

                    centre = {(z, r): u_at(z, r, 0) for z in parts for r in rows}
                    ups = {c: pltpu.roll(u, LANES - 1, 1) for c, u in centre.items()}
                    downs = {c: pltpu.roll(u, 1, 1) for c, u in centre.items()}
                    total = {}
                    for z in parts:
                        col = [u_at(z, -1, 0)] + [centre[z, r] for r in rows] + [u_at(z, count, 0)]
                        act = [a_at(z, i, 0) for i in range(-1, count + 1)]
                        flux = [(act[i] + act[i + 1]) * (col[i + 1] - col[i]) for i in range(count + 1)]
                        for r in rows:
                            uc, ac = col[r + 1], act[r + 1]
                            up = (ac + a_at(z, r, 1)) * (u_at(z, r, 1) - uc)
                            moved = pltpu.roll(up, 1, 0)
                            if k:
                                down = jnp.where(line == 0, below_flux[n, z, r], moved)
                            else:
                                down = (ac + a_at(z, r, -1)) * (uc - u_at(z, r, -1))
                            below_flux[n, z, r] = moved
                            spread = (flux[r + 1] - flux[r]) + (up - down)
                            near_x = merge(edges, [u_at(z, r - s, 0) for s in step_x])
                            far_x = merge(edges, [u_at(z, r - 2 * s, 0) for s in step_x])
                            near_y = merge(edges, [u_at(z, r, -s) for s in step_y])
                            far_y = merge(edges, [u_at(z, r, -2 * s) for s in step_y])
                            total[z, r] = ((strength * spread + c3[z] * uc) + cx[z] * (far_x - 4.0 * near_x)
                                           + cy[z] * (far_y - 4.0 * near_y))
                    for r in rows:
                        for z in parts:
                            u = centre[z, r]
                            above = jnp.where(top, ups[z + 1, r] if z + 1 < halves else u, ups[z, r])
                            below = jnp.where(bottom, downs[z - 1, r] if z else u, downs[z, r])
                            bend = (above - u) + (below - u)
                            rate = total[z, r] + mix[z, x + r, pl.ds(y, TILE), :] * bend
                            rates[n, z, r] = rate

                            def get(ref, m=n):
                                return ref[m, z, x + r, pl.ds(y, TILE), :]

                            def put(ref, value):
                                puts.append((ref, (n, z, x + r, y), value))
                            finish(get, put, n, rates.get((n - 1, z, r), rate), u, rate)
            for ref, at, value in puts:
                write(ref, at, value)

        for tiles, column, near, far in row_classes(reach, own_columns):
            if near == 0:
                group = 4 if own_rows % 4 == 0 else 2

                @pl.loop(0, own_rows // group)
                def _(i, column=column, tiles=tiles, group=group):
                    block(HALO + group * i, group, column, tiles)
            else:
                span = 2 * (far - near + 1)
                group = 4 if span % 4 == 0 else 2
                width = span // group

                @pl.loop(0, 2 * width, unroll=2 if group == 2 else 1)
                def _(i, column=column, tiles=tiles, near=near, far=far, width=width, group=group):
                    low = HALO - 2 * far + group * i
                    high = HALO + own_rows + 2 * (near - 1) + group * (i - width)
                    block(jnp.where(i < width, low, high), group, column, tiles)

    w1 = [time_step / half_step * w for w in first_weights]
    w2 = [time_step / half_step * w for w in second_weights]
    assert abs(sum(w1) - 1) < 1e-12 and abs(sum(w2) - 1) < 1e-12

    def end_1(get, put, n, earlier, u, rate):
        m = get(start, max(n - 1, 0)) + ((earlier - rate) + rate)
        put(f, rate)
        put(mid, m)
        put(act_b, growth(m))

    def end_2(get, put, n, earlier, u, rate):
        first = get(f)
        last = u + ((rate - first) + first)
        put(g1, rate)
        put(last_1, last)
        put(act_a, growth(last))

    def end_3(get, put, n, earlier, u, rate):
        begin = get(last_1, n - 1) if n else get(start, 0)
        g0 = earlier if n else get(f, 0)
        m = begin + g0 + (w1[0] - 1.0) * get(f, max(n - 1, 0)) + w1[1] * get(g1) + w1[2] * rate
        put(g2, rate)
        put(mid, m)
        put(act_b, growth(m))

    def end_4(get, put, n, earlier, u, rate):
        last = u + rate + w2[0] * get(f, max(n - 1, 0)) + (w2[1] - 1.0) * get(g1) + w2[2] * get(g2)
        put(g1b, rate)
        put(last_2, last)
        put(act_a, growth(last))

    def end_5(get, put, n, earlier, u, rate):
        begin = get(last_2, n - 1) if n else get(start, 0)
        g0 = earlier if n else get(f, 0)
        before = get(g2, n - 1) if n else get(f, 0)
        m = begin + g0 + (w1[0] - 1.0) * before + w1[1] * get(g1b) + w1[2] * rate
        put(g2b, rate)
        put(mid, m)
        put(act_b, growth(m))

    def end_6(get, put, n, earlier, u, rate):
        before = get(g2, n - 1) if n else get(f, 0)
        put("middle", u)
        put("final", u + rate + w2[0] * before + (w2[1] - 1.0) * get(g1b) + w2[2] * get(g2b))

    evaluate(10, start, act_a, end_1)
    evaluate(8, mid, act_b, end_2)
    evaluate(6, last_1, act_a, end_3)
    evaluate(4, mid, act_b, end_4)
    evaluate(2, last_2, act_a, end_5)
    evaluate(0, mid, act_b, end_6)


def outside(word, low_x, low_y):
    return jnp.where(word == 0, 8 + (0 if low_x else 1) + (0 if low_y else 2), word - 1)


DEPTHS = (HALO, HALO, HALO - 2)


def corner_rows():
    out, offset = [], 0
    for a, depth in enumerate(DEPTHS):
        for d in range(depth - 2):
            wide = depth - 2 * (d // 2 + 1)
            out.append((a, d, offset, wide))
            offset += wide
    return out, offset


CORNER_ROWS, CORNER_SIZE = corner_rows()
BEFORE = tuple(sum(DEPTHS[:a]) for a in range(len(DEPTHS) + 1))


def pack_kernel(where_ref, code, own, other, mixing, beside_x, beside_y, diagonal_1, diagonal_2):
    t = where_ref[0]
    rows, columns, levels = own.shape
    word = jnp.full((TILE, LANES), (code[0, 0] + 1).astype(jnp.float32))
    for ref in (beside_x, beside_y, diagonal_1, diagonal_2):
        ref[0, pl.ds(ref.shape[1] - TILE, TILE), :] = word

    def side(low):
        arrays = (own, other, mixing) if low else (other, own, mixing)
        for z in range(levels // LANES):
            lanes = pl.ds(z * LANES, LANES)
            for a, depth in enumerate(DEPTHS):
                for i in range(depth):
                    x = i if low else rows - depth + i
                    beside_x[z, pl.ds((BEFORE[a] + i) * columns, columns), :] = arrays[a][x, :, lanes]
            for a, d, offset, wide in CORNER_ROWS:
                x = d if low else rows - 1 - d
                near, far = arrays[a][x, pl.ds(0, wide), lanes], arrays[a][x, pl.ds(columns - wide, wide), lanes]
                diagonal_1[z, pl.ds(offset, wide), :] = near if low else far
                diagonal_2[z, pl.ds(offset, wide), :] = far if low else near

        @pl.loop(0, rows // 2)
        def _(i):
            for x in (2 * i, 2 * i + 1):
                for z in range(levels // LANES):
                    for a, depth in enumerate(DEPTHS):
                        line = arrays[a][x, pl.ds(0 if low else columns - depth, depth), pl.ds(z * LANES, LANES)]
                        beside_y[z, pl.ds(BEFORE[a] * rows + x * depth, depth), :] = line

    pl.when(t == 0)(lambda: side(True))
    pl.when(t != 0)(lambda: side(False))


def pair_kernel(where_ref, code, wind, own, other, mixing, halo_x, halo_y, passed_y, corner_1, corner_2,
                mine_middle, mine_final, theirs, start, mid, last_1, last_2, f, g1, g1b, g2, g2b, act_a, act_b,
                mix, both, codes):
    t = where_ref[0]
    block_rows, columns, levels = own.shape
    halves = levels // LANES
    half = block_rows // 2
    inner = half + HALO

    def word_of(ref):
        return jnp.max(ref[0, pl.ds(ref.shape[1] - TILE, TILE), :]).astype(jnp.int32)

    word_x, word_y, word_p, word_1, word_2 = [word_of(r) for r in (halo_x, halo_y, passed_y, corner_1, corner_2)]

    def fill(a, z, x, y, value):
        at = (z, x, pl.ds(y, value.shape[0]), slice(None))
        if a < 2:
            start[(a, *at)] = value
            act_a[(a, *at)] = growth(value)
        else:
            mix[at] = half_step * value

    def side(low):
        at_own, from_own, at_x = (HALO, 0, 0) if low else (0, block_rows - inner, inner)
        low_y, high_y = (halo_y, passed_y) if low else (passed_y, halo_y)
        low_corner, high_corner = (corner_1, corner_2) if low else (corner_2, corner_1)
        word_low, word_high = (word_y, word_p) if low else (word_p, word_y)
        corner_low, corner_high = (word_1, word_2) if low else (word_2, word_1)
        arrays = (own, other, mixing) if low else (other, own, mixing)

        @pl.loop(0, inner)
        def _(i):
            codes[(at_own + i) * 3] = outside(word_low, True, True)
            codes[(at_own + i) * 3 + 1] = code[0, 0]
            codes[(at_own + i) * 3 + 2] = outside(word_high, True, False)

        @pl.loop(0, HALO)
        def _(i):
            codes[(at_x + i) * 3] = outside(corner_low, low, True)
            codes[(at_x + i) * 3 + 1] = outside(word_x, low, True)
            codes[(at_x + i) * 3 + 2] = outside(corner_high, low, False)

        @pl.loop(0, inner // 2)
        def _(pair):
            for i in (2 * pair, 2 * pair + 1):
                x = from_own + i
                for z in range(halves):
                    for a, depth in enumerate(DEPTHS):
                        for y in range(0, columns, TILE):
                            fill(a, z, at_own + i, HALO + y, arrays[a][x, pl.ds(y, TILE), pl.ds(z * LANES, LANES)])
                        at = pl.ds(BEFORE[a] * block_rows + x * depth, depth)
                        fill(a, z, at_own + i, HALO - depth, low_y[z, at, :])
                        fill(a, z, at_own + i, HALO + columns, high_y[z, at, :])

        for z in range(halves):
            for a, depth in enumerate(DEPTHS):
                for i in range(depth):
                    x = HALO - depth + i if low else inner + i
                    for y in range(0, columns, TILE):
                        fill(a, z, x, HALO + y, halo_x[z, pl.ds((BEFORE[a] + i) * columns + y, TILE), :])
            for a, d, offset, wide in CORNER_ROWS:
                x = HALO - 1 - d if low else inner + d
                fill(a, z, x, HALO - wide, low_corner[z, pl.ds(offset, wide), :])
                fill(a, z, x, HALO + columns, high_corner[z, pl.ds(offset, wide), :])

    pl.when(t == 0)(lambda: side(True))
    pl.when(t != 0)(lambda: side(False))

    def write(ref, at, value):
        n, z, x, y = at
        if isinstance(ref, str):
            place = jnp.where(t == n, 0, 1)
            both[place, 0 if ref == "middle" else 1, x - HALO, pl.ds(y - HALO, TILE), pl.ds(z * LANES, LANES)] = value
        else:
            ref[n, z, x, pl.ds(y, TILE), :] = value

    sweeps(half, columns, codes, wind, mix, start, mid, last_1, last_2, f, g1, g1b, g2, g2b, act_a, act_b, write)
    here = pl.ds(t * half, half)
    mine_middle[here] = both[0, 0]
    mine_final[here] = both[0, 1]
    theirs[...] = both[1]


VMEM = pl.BlockSpec(memory_space=pltpu.VMEM)
SMEM = pl.BlockSpec(memory_space=pltpu.SMEM)
LIMIT = 56 * 2**20


def of(*shape):
    return jax.ShapeDtypeStruct(shape, jnp.float32)


def near(x):
    return pltpu.with_memory_space_constraint(x, pltpu.VMEM)


def pair_shards(state, code, wind, mixing, sizes):
    axes = ("tm", "gx", "gy")
    rows, columns, levels = state.shape
    halves = levels // LANES
    t = lax.axis_index("tm")
    where = t.astype(jnp.int32).reshape(1)

    def partners(step_x, step_y):
        pairs = []
        for x in range(sizes[1]):
            for y in range(sizes[2]):
                u, v = x - step_x, y - step_y
                if 0 <= u < sizes[1] and 0 <= v < sizes[2]:
                    here, there = x * sizes[2] + y, (sizes[1] + u) * sizes[2] + v
                    pairs += [(here, there), (there, here)]
        return pairs

    swap = [(0, 1), (1, 0)]
    other = near(lax.ppermute(state, "tm", swap))
    corner = (halves, CORNER_SIZE + TILE, LANES)
    to_x, to_y, to_1, to_2 = pl.pallas_call(
        pack_kernel,
        out_shape=[pltpu.VMEM(s, jnp.float32) for s in (
            (halves, BEFORE[-1] * columns + TILE, LANES), (halves, BEFORE[-1] * rows + TILE, LANES), corner, corner)],
        in_specs=[SMEM, SMEM, VMEM, VMEM, VMEM], out_specs=[VMEM] * 4,
        compiler_params=pltpu.CompilerParams(vmem_limit_bytes=LIMIT),
    )(where, code, state, other, mixing)
    halo_x = lax.ppermute(to_x, axes, partners(1, 0))
    halo_y = lax.ppermute(to_y, axes, partners(0, 1))
    corner_1 = lax.ppermute(to_1, axes, partners(1, 1))
    corner_2 = lax.ppermute(to_2, axes, partners(1, -1))
    halo_x, halo_y, corner_1, corner_2 = lax.optimization_barrier((halo_x, halo_y, corner_1, corner_2))
    passed_y = lax.ppermute(halo_y, "tm", swap)
    halo_x, halo_y, passed_y, corner_1, corner_2 = map(near, (halo_x, halo_y, passed_y, corner_1, corner_2))
    half = rows // 2
    plane = (halves, half + 2 * HALO, columns + 2 * HALO + TILE, LANES)
    middle, final, theirs = pl.pallas_call(
        pair_kernel, out_shape=(of(*state.shape), of(*state.shape), pltpu.VMEM((2, half, columns, levels), jnp.float32)),
        in_specs=[SMEM, SMEM] + [VMEM] * 9, out_specs=[VMEM] * 3,
        scratch_shapes=[pltpu.VMEM((2, *plane), jnp.float32)] * 11 + [
            pltpu.VMEM(plane, jnp.float32), pltpu.VMEM((2, 2, half, columns, levels), jnp.float32),
            pltpu.SMEM((3 * (half + 2 * HALO),), jnp.int32)],
        compiler_params=pltpu.CompilerParams(vmem_limit_bytes=LIMIT),
    )(where, code, wind, state, other, mixing, halo_x, halo_y, passed_y, corner_1, corner_2)
    got = lax.ppermute(theirs, "tm", swap)
    there = ((1 - t) * half, 0, 0)
    return lax.dynamic_update_slice(middle, got[0], there)[None], lax.dynamic_update_slice(final, got[1], there)[None]


def padded(x, sides, width):
    for axis, dim in sides:
        devices, length = lax.axis_size(axis), x.shape[dim]
        up = [(i, i + 1) for i in range(devices - 1)]
        down = [(j, i) for i, j in up]
        before = lax.ppermute(lax.slice_in_dim(x, length - width, length, axis=dim), axis, up)
        after = lax.ppermute(lax.slice_in_dim(x, 0, width, axis=dim), axis, down)
        x = jnp.concatenate([before, x, after], axis=dim)
    return x


def tendency(u, sign_x, sign_y, strength, wind, mixing):
    rows, columns = mixing.shape[:2]

    def beside(source, step_x, step_y):
        return source[2 + step_x:2 + step_x + rows, 2 + step_y:2 + step_y + columns]

    centre = beside(u, 0, 0)
    act = 0.5 * growth(u)
    spread = sum((beside(act, 0, 0) + beside(act, *s)) * (beside(u, *s) - centre) for s in ((1, 0), (-1, 0), (0, 1), (0, -1)))
    near_x, far_x = (jnp.where(sign_x > 0, beside(u, -k, 0), beside(u, k, 0)) for k in (1, 2))
    near_y, far_y = (jnp.where(sign_y > 0, beside(u, 0, -k), beside(u, 0, k)) for k in (1, 2))
    carried = wind[0] * (3.0 * centre - 4.0 * near_x + far_x) + wind[1] * (3.0 * centre - 4.0 * near_y + far_y)
    below = jnp.concatenate([centre[:, :, :1], centre[:, :, :-1]], axis=2)
    above = jnp.concatenate([centre[:, :, 1:], centre[:, :, -1:]], axis=2)
    return strength * spread - 0.5 * carried + mixing * (below + above - 2.0 * centre)


def slice_shards(state, code, wind, mixing, sizes):
    word = code[0, 0]
    strength = jnp.where(word // 4 == 1, diffusion_high, diffusion_low)

    def rate_of(u):
        return tendency(padded(u, (("gx", 0), ("gy", 1)), 2), 1 - 2 * (word % 2), 1 - 2 * (word // 2 % 2), strength, wind, mixing)

    start_rate = rate_of(state)
    last, rates = state, (start_rate,) * 3
    for _ in range(SWEEPS):
        arrived = lax.ppermute((last, rates[2]), "tm", [(i, i + 1) for i in range(sizes[0] - 1)])
        first, g0 = (jnp.where(lax.axis_index("tm") == 0, a, b) for a, b in zip((state, start_rate), arrived))
        middle = first + half_step * (g0 - rates[0]) + time_step * sum(w * r for w, r in zip(first_weights, rates))
        g1 = rate_of(middle)
        last = middle + half_step * (g1 - rates[1]) + time_step * sum(w * r for w, r in zip(second_weights, rates))
        rates = g0, g1, rate_of(last)
    return middle[None], last[None]


def solution(mesh):
    sizes = tuple(mesh.shape[a] for a in ("tm", "gx", "gy"))
    run = pair_shards if sizes[0] == 2 else slice_shards

    def shards(start_states, wind_code, wind_profile, vertical_mix):
        return run(start_states[0], wind_code, wind_profile, vertical_mix, sizes)

    in_specs = (P("tm", "gx", "gy", None), P("gx", "gy"), P(), P("gx", "gy", None))
    out_specs = (P("tm", "gx", "gy", None), P("tm", "gx", "gy", None))
    return jax.shard_map(shards, mesh=mesh, in_specs=in_specs, out_specs=out_specs, check_vma=False)
```

```python
import functools
import jax
import jax.numpy as jnp
from jax import lax
from jax.experimental import pallas as pl
from jax.experimental.pallas import tpu as pltpu
from jax.sharding import PartitionSpec as P

SWEEPS = 3
HALO = 4 * SWEEPS
LANES = 128
TILE = 8
time_step = 0.5
half_step = 0.25
diffusion_low = 0.04
diffusion_high = 0.1
first_weights = (5.0 / 24.0, 1.0 / 3.0, -1.0 / 24.0)
second_weights = (-1.0 / 24.0, 1.0 / 3.0, 5.0 / 24.0)


def row_classes(reach, own):
    steps = reach // 2
    groups = {}
    for a in range(steps + 1):
        beside = 2 * (steps - a) if a else reach
        groups.setdefault((-(-(own + 2 * beside) // TILE), a == 0), []).append((a, beside))
    out = []
    for (tiles, _), members in sorted(groups.items()):
        beside = max(b for _, b in members)
        begins = range(max(2, HALO + own + beside - TILE * tiles), HALO - beside + 1)
        cuts = lambda begin: sum(begin < e < begin + TILE * tiles and (e - begin) % TILE > 0 for e in (HALO, HALO + own))
        out.append((tiles, min(begins, key=cuts), members[0][0], members[-1][0]))
    return out


def growth(u):
    return 1.5 - 1.0 / (1.0 + u * u)


def sweeps(own_rows, own_columns, codes, wind, mix, start, mid, last_1, last_2, f, g1, g1b, g2, g2b, act_a, act_b,
           write):
    halves = mix.shape[0]
    slices, parts = range(start.shape[0]), range(halves)
    scale = 0.5 * half_step
    lane = lax.broadcasted_iota(jnp.int32, (TILE, LANES), 1)
    line = lax.broadcasted_iota(jnp.int32, (TILE, LANES), 0)
    bottom, top = lane == 0, lane == LANES - 1
    cx = [jnp.broadcast_to(-0.5 * half_step * wind[0:1, z * LANES:(z + 1) * LANES], (TILE, LANES)) for z in parts]
    cy = [jnp.broadcast_to(-0.5 * half_step * wind[1:2, z * LANES:(z + 1) * LANES], (TILE, LANES)) for z in parts]
    c3 = [3.0 * (a + b) for a, b in zip(cx, cy)]

    def merge(edges, values):
        got = values[-1]
        for e, value in zip(reversed(edges), reversed(values[:-1])):
            got = jnp.where(line < e, value, got)
        return got

    def evaluate(reach, source, active, finish):
        def block(x, count, column, tiles):
            rows = range(count)
            puts, below_flux = [], {}
            for k in range(tiles):
                y = column + TILE * k
                edges = [e - y for e in (HALO, HALO + own_columns) if y < e < y + TILE]
                sides = [sum(p >= e for e in (HALO, HALO + own_columns)) for p in [y] + [y + e for e in edges]]
                words = [codes[x * 3 + j] for j in sides]
                kh = [jnp.where(w >= 8, 0.0, jnp.where(w >= 4, scale * diffusion_high, scale * diffusion_low)) for w in words]
                step_x = [1 - 2 * (w & 1) for w in words]
                step_y = [1 - (w & 2) for w in words]
                strength = merge(edges, [jnp.full((TILE, LANES), s, jnp.float32) for s in kh])
                rates = {}
                for n in slices:
                    def u_at(z, i, j):
                        return source[n, z, x + i, pl.ds(y + j, TILE), :]

                    def a_at(z, i, j):
                        return active[n, z, x + i, pl.ds(y + j, TILE), :]

                    centre = {(z, r): u_at(z, r, 0) for z in parts for r in rows}
                    ups = {c: pltpu.roll(u, LANES - 1, 1) for c, u in centre.items()}
                    downs = {c: pltpu.roll(u, 1, 1) for c, u in centre.items()}
                    total = {}
                    for z in parts:
                        col = [u_at(z, -1, 0)] + [centre[z, r] for r in rows] + [u_at(z, count, 0)]
                        act = [a_at(z, i, 0) for i in range(-1, count + 1)]
                        flux = [(act[i] + act[i + 1]) * (col[i + 1] - col[i]) for i in range(count + 1)]
                        for r in rows:
                            uc, ac = col[r + 1], act[r + 1]
                            up = (ac + a_at(z, r, 1)) * (u_at(z, r, 1) - uc)
                            moved = pltpu.roll(up, 1, 0)
                            if k:
                                down = jnp.where(line == 0, below_flux[n, z, r], moved)
                            else:
                                down = (ac + a_at(z, r, -1)) * (uc - u_at(z, r, -1))
                            below_flux[n, z, r] = moved
                            spread = (flux[r + 1] - flux[r]) + (up - down)
                            near_x = merge(edges, [u_at(z, r - s, 0) for s in step_x])
                            far_x = merge(edges, [u_at(z, r - 2 * s, 0) for s in step_x])
                            near_y = merge(edges, [u_at(z, r, -s) for s in step_y])
                            far_y = merge(edges, [u_at(z, r, -2 * s) for s in step_y])
                            total[z, r] = ((strength * spread + c3[z] * uc) + cx[z] * (far_x - 4.0 * near_x)
                                           + cy[z] * (far_y - 4.0 * near_y))
                    for r in rows:
                        for z in parts:
                            u = centre[z, r]
                            above = jnp.where(top, ups[z + 1, r] if z + 1 < halves else u, ups[z, r])
                            below = jnp.where(bottom, downs[z - 1, r] if z else u, downs[z, r])
                            bend = (above - u) + (below - u)
                            rate = total[z, r] + mix[z, x + r, pl.ds(y, TILE), :] * bend
                            rates[n, z, r] = rate

                            def get(ref, m=n):
                                return ref[m, z, x + r, pl.ds(y, TILE), :]

                            def put(ref, value):
                                puts.append((ref, (n, z, x + r, y), value))
                            finish(get, put, n, rates.get((n - 1, z, r), rate), u, rate)
            for ref, at, value in puts:
                write(ref, at, value)

        for tiles, column, near, far in row_classes(reach, own_columns):
            if near == 0:
                group = 4 if own_rows % 4 == 0 else 2

                @pl.loop(0, own_rows // group)
                def _(i, column=column, tiles=tiles, group=group):
                    block(HALO + group * i, group, column, tiles)
            else:
                span = 2 * (far - near + 1)
                group = 4 if span % 4 == 0 else 2
                width = span // group

                @pl.loop(0, 2 * width, unroll=2 if group == 2 else 1)
                def _(i, column=column, tiles=tiles, near=near, far=far, width=width, group=group):
                    low = HALO - 2 * far + group * i
                    high = HALO + own_rows + 2 * (near - 1) + group * (i - width)
                    block(jnp.where(i < width, low, high), group, column, tiles)

    w1 = [time_step / half_step * w for w in first_weights]
    w2 = [time_step / half_step * w for w in second_weights]
    assert abs(sum(w1) - 1) < 1e-12 and abs(sum(w2) - 1) < 1e-12

    def end_1(get, put, n, earlier, u, rate):
        m = get(start, max(n - 1, 0)) + ((earlier - rate) + rate)
        put(f, rate)
        put(mid, m)
        put(act_b, growth(m))

    def end_2(get, put, n, earlier, u, rate):
        first = get(f)
        last = u + ((rate - first) + first)
        put(g1, rate)
        put(last_1, last)
        put(act_a, growth(last))

    def end_3(get, put, n, earlier, u, rate):
        begin = get(last_1, n - 1) if n else get(start, 0)
        g0 = earlier if n else get(f, 0)
        m = begin + g0 + (w1[0] - 1.0) * get(f, max(n - 1, 0)) + w1[1] * get(g1) + w1[2] * rate
        put(g2, rate)
        put(mid, m)
        put(act_b, growth(m))

    def end_4(get, put, n, earlier, u, rate):
        last = u + rate + w2[0] * get(f, max(n - 1, 0)) + (w2[1] - 1.0) * get(g1) + w2[2] * get(g2)
        put(g1b, rate)
        put(last_2, last)
        put(act_a, growth(last))

    def end_5(get, put, n, earlier, u, rate):
        begin = get(last_2, n - 1) if n else get(start, 0)
        g0 = earlier if n else get(f, 0)
        before = get(g2, n - 1) if n else get(f, 0)
        m = begin + g0 + (w1[0] - 1.0) * before + w1[1] * get(g1b) + w1[2] * rate
        put(g2b, rate)
        put(mid, m)
        put(act_b, growth(m))

    def end_6(get, put, n, earlier, u, rate):
        before = get(g2, n - 1) if n else get(f, 0)
        put("middle", u)
        put("final", u + rate + w2[0] * before + (w2[1] - 1.0) * get(g1b) + w2[2] * get(g2b))

    evaluate(10, start, act_a, end_1)
    evaluate(8, mid, act_b, end_2)
    evaluate(6, last_1, act_a, end_3)
    evaluate(4, mid, act_b, end_4)
    evaluate(2, last_2, act_a, end_5)
    evaluate(0, mid, act_b, end_6)


def outside(word, low_x, low_y):
    return jnp.where(word == 0, 8 + (0 if low_x else 1) + (0 if low_y else 2), word - 1)


DEPTHS = (HALO, HALO, HALO - 2)


def corner_rows():
    out, offset = [], 0
    for a, depth in enumerate(DEPTHS):
        for d in range(depth - 2):
            wide = depth - 2 * (d // 2 + 1)
            out.append((a, d, offset, wide))
            offset += wide
    return out, offset


CORNER_ROWS, CORNER_SIZE = corner_rows()
BEFORE = tuple(sum(DEPTHS[:a]) for a in range(len(DEPTHS) + 1))


def load_kernel(state, mixing, state_near, mixing_near, semaphores):
    made = [pltpu.make_async_copy(a, b, semaphores.at[k])
            for k, (a, b) in enumerate(((state, state_near), (mixing, mixing_near)))]
    for one in made:
        one.start()
    for one in made:
        one.wait()


def pack_kernel(where_ref, code, own, other, mixing, beside_x, beside_y, diagonal_1, diagonal_2):
    t = where_ref[0]
    rows, columns, levels = own.shape
    word = jnp.full((TILE, LANES), (code[0, 0] + 1).astype(jnp.float32))
    for ref in (beside_x, beside_y, diagonal_1, diagonal_2):
        ref[0, pl.ds(ref.shape[1] - TILE, TILE), :] = word

    def side(low):
        arrays = (own, other, mixing) if low else (other, own, mixing)
        for z in range(levels // LANES):
            lanes = pl.ds(z * LANES, LANES)
            for a, depth in enumerate(DEPTHS):
                for i in range(depth):
                    x = i if low else rows - depth + i
                    beside_x[z, pl.ds((BEFORE[a] + i) * columns, columns), :] = arrays[a][x, :, lanes]
            for a, d, offset, wide in CORNER_ROWS:
                x = d if low else rows - 1 - d
                near, far = arrays[a][x, pl.ds(0, wide), lanes], arrays[a][x, pl.ds(columns - wide, wide), lanes]
                diagonal_1[z, pl.ds(offset, wide), :] = near if low else far
                diagonal_2[z, pl.ds(offset, wide), :] = far if low else near

        @pl.loop(0, rows // 2)
        def _(i):
            for x in (2 * i, 2 * i + 1):
                for z in range(levels // LANES):
                    for a, depth in enumerate(DEPTHS):
                        line = arrays[a][x, pl.ds(0 if low else columns - depth, depth), pl.ds(z * LANES, LANES)]
                        beside_y[z, pl.ds(BEFORE[a] * rows + x * depth, depth), :] = line

    pl.when(t == 0)(lambda: side(True))
    pl.when(t != 0)(lambda: side(False))


def pair_kernel(where_ref, code, wind, own, other, mixing, halo_x, halo_y, passed_y, corner_1, corner_2,
                mine, theirs, start, mid, last_1, last_2, f, g1, g1b, g2, g2b, act_a, act_b,
                mix, both, codes):
    t = where_ref[0]
    block_rows, columns, levels = own.shape
    halves = levels // LANES
    half = block_rows // 2
    inner = half + HALO

    def word_of(ref):
        return jnp.max(ref[0, pl.ds(ref.shape[1] - TILE, TILE), :]).astype(jnp.int32)

    word_x, word_y, word_p, word_1, word_2 = [word_of(r) for r in (halo_x, halo_y, passed_y, corner_1, corner_2)]

    def fill(a, z, x, y, value):
        at = (z, x, pl.ds(y, value.shape[0]), slice(None))
        if a < 2:
            start[(a, *at)] = value
            act_a[(a, *at)] = growth(value)
        else:
            mix[at] = half_step * value

    def side(low):
        at_own, from_own, at_x = (HALO, 0, 0) if low else (0, block_rows - inner, inner)
        low_y, high_y = (halo_y, passed_y) if low else (passed_y, halo_y)
        low_corner, high_corner = (corner_1, corner_2) if low else (corner_2, corner_1)
        word_low, word_high = (word_y, word_p) if low else (word_p, word_y)
        corner_low, corner_high = (word_1, word_2) if low else (word_2, word_1)
        arrays = (own, other, mixing) if low else (other, own, mixing)

        @pl.loop(0, inner)
        def _(i):
            codes[(at_own + i) * 3] = outside(word_low, True, True)
            codes[(at_own + i) * 3 + 1] = code[0, 0]
            codes[(at_own + i) * 3 + 2] = outside(word_high, True, False)

        @pl.loop(0, HALO)
        def _(i):
            codes[(at_x + i) * 3] = outside(corner_low, low, True)
            codes[(at_x + i) * 3 + 1] = outside(word_x, low, True)
            codes[(at_x + i) * 3 + 2] = outside(corner_high, low, False)

        @pl.loop(0, inner // 2)
        def _(pair):
            for i in (2 * pair, 2 * pair + 1):
                x = from_own + i
                for z in range(halves):
                    for a, depth in enumerate(DEPTHS):
                        for y in range(0, columns, TILE):
                            fill(a, z, at_own + i, HALO + y, arrays[a][x, pl.ds(y, TILE), pl.ds(z * LANES, LANES)])
                        at = pl.ds(BEFORE[a] * block_rows + x * depth, depth)
                        fill(a, z, at_own + i, HALO - depth, low_y[z, at, :])
                        fill(a, z, at_own + i, HALO + columns, high_y[z, at, :])

        for z in range(halves):
            for a, depth in enumerate(DEPTHS):
                for i in range(depth):
                    x = HALO - depth + i if low else inner + i
                    for y in range(0, columns, TILE):
                        fill(a, z, x, HALO + y, halo_x[z, pl.ds((BEFORE[a] + i) * columns + y, TILE), :])
            for a, d, offset, wide in CORNER_ROWS:
                x = HALO - 1 - d if low else inner + d
                fill(a, z, x, HALO - wide, low_corner[z, pl.ds(offset, wide), :])
                fill(a, z, x, HALO + columns, high_corner[z, pl.ds(offset, wide), :])

    pl.when(t == 0)(lambda: side(True))
    pl.when(t != 0)(lambda: side(False))

    def write(ref, at, value):
        n, z, x, y = at
        if isinstance(ref, str):
            place = jnp.where(t == n, 0, 1)
            both[place, 0 if ref == "middle" else 1, x - HALO, pl.ds(y - HALO, TILE), pl.ds(z * LANES, LANES)] = value
        else:
            ref[n, z, x, pl.ds(y, TILE), :] = value

    sweeps(half, columns, codes, wind, mix, start, mid, last_1, last_2, f, g1, g1b, g2, g2b, act_a, act_b, write)
    mine[...] = both[0]
    theirs[...] = both[1]


def merge_kernel(where_ref, mine, got, middle, final, semaphores):
    t = where_ref[0]
    half = mine.shape[1]

    def merge(low):
        halves = (mine, got) if low else (got, mine)
        made = [pltpu.make_async_copy(part.at[k], out.at[pl.ds(h * half, half)], semaphores.at[2 * h + k])
                for h, part in enumerate(halves) for k, out in enumerate((middle, final))]
        for one in made:
            one.start()
        for one in made:
            one.wait()

    pl.when(t == 0)(lambda: merge(True))
    pl.when(t != 0)(lambda: merge(False))


VMEM = pl.BlockSpec(memory_space=pltpu.VMEM)
SMEM = pl.BlockSpec(memory_space=pltpu.SMEM)
ANY = pl.BlockSpec(memory_space=pl.ANY)
LIMIT = 56 * 2**20


def of(*shape):
    return jax.ShapeDtypeStruct(shape, jnp.float32)


def near(x):
    return pltpu.with_memory_space_constraint(x, pltpu.VMEM)


def pair_shards(state, code, wind, mixing, sizes):
    axes = ("tm", "gx", "gy")
    rows, columns, levels = state.shape
    halves = levels // LANES
    t = lax.axis_index("tm")
    where = t.astype(jnp.int32).reshape(1)

    def partners(step_x, step_y):
        pairs = []
        for x in range(sizes[1]):
            for y in range(sizes[2]):
                u, v = x - step_x, y - step_y
                if 0 <= u < sizes[1] and 0 <= v < sizes[2]:
                    here, there = x * sizes[2] + y, (sizes[1] + u) * sizes[2] + v
                    pairs += [(here, there), (there, here)]
        return pairs

    swap = [(0, 1), (1, 0)]
    other = near(lax.ppermute(state, "tm", swap))
    state, mixing = pl.pallas_call(
        load_kernel, out_shape=[pltpu.VMEM(x.shape, jnp.float32) for x in (state, mixing)],
        in_specs=[ANY] * 2, out_specs=[VMEM] * 2, scratch_shapes=[pltpu.SemaphoreType.DMA((2,))],
        cost_estimate=pl.CostEstimate(flops=0, bytes_accessed=16 * state.size, transcendentals=0),
    )(state, mixing)
    state, mixing = near(state), near(mixing)
    corner = (halves, CORNER_SIZE + TILE, LANES)
    to_x, to_y, to_1, to_2 = pl.pallas_call(
        pack_kernel,
        out_shape=[pltpu.VMEM(s, jnp.float32) for s in (
            (halves, BEFORE[-1] * columns + TILE, LANES), (halves, BEFORE[-1] * rows + TILE, LANES), corner, corner)],
        in_specs=[SMEM, SMEM, VMEM, VMEM, VMEM], out_specs=[VMEM] * 4,
        compiler_params=pltpu.CompilerParams(vmem_limit_bytes=LIMIT),
    )(where, code, state, other, mixing)
    halo_x = lax.ppermute(to_x, axes, partners(1, 0))
    halo_y = lax.ppermute(to_y, axes, partners(0, 1))
    corner_1 = lax.ppermute(to_1, axes, partners(1, 1))
    corner_2 = lax.ppermute(to_2, axes, partners(1, -1))
    halo_x, halo_y, corner_1, corner_2 = lax.optimization_barrier((halo_x, halo_y, corner_1, corner_2))
    passed_y = lax.ppermute(halo_y, "tm", swap)
    halo_x, halo_y, passed_y, corner_1, corner_2 = map(near, (halo_x, halo_y, passed_y, corner_1, corner_2))
    half = rows // 2
    plane = (halves, half + 2 * HALO, columns + 2 * HALO + TILE, LANES)
    mine, theirs = pl.pallas_call(
        pair_kernel, out_shape=[pltpu.VMEM((2, half, columns, levels), jnp.float32)] * 2,
        in_specs=[SMEM, SMEM] + [VMEM] * 9, out_specs=[VMEM] * 2,
        scratch_shapes=[pltpu.VMEM((2, *plane), jnp.float32)] * 11 + [
            pltpu.VMEM(plane, jnp.float32), pltpu.VMEM((2, 2, half, columns, levels), jnp.float32),
            pltpu.SMEM((3 * (half + 2 * HALO),), jnp.int32)],
        compiler_params=pltpu.CompilerParams(vmem_limit_bytes=LIMIT),
    )(where, code, wind, state, other, mixing, halo_x, halo_y, passed_y, corner_1, corner_2)
    got = lax.ppermute(theirs, "tm", swap)
    middle, final = pl.pallas_call(
        merge_kernel, out_shape=[of(*state.shape)] * 2, in_specs=[SMEM, VMEM, VMEM], out_specs=[ANY] * 2,
        scratch_shapes=[pltpu.SemaphoreType.DMA((4,))],
    )(where, near(mine), near(got))
    return middle[None], final[None]


def padded(x, sides, width):
    for axis, dim in sides:
        devices, length = lax.axis_size(axis), x.shape[dim]
        up = [(i, i + 1) for i in range(devices - 1)]
        down = [(j, i) for i, j in up]
        before = lax.ppermute(lax.slice_in_dim(x, length - width, length, axis=dim), axis, up)
        after = lax.ppermute(lax.slice_in_dim(x, 0, width, axis=dim), axis, down)
        x = jnp.concatenate([before, x, after], axis=dim)
    return x


def tendency(u, sign_x, sign_y, strength, wind, mixing):
    rows, columns = mixing.shape[:2]

    def beside(source, step_x, step_y):
        return source[2 + step_x:2 + step_x + rows, 2 + step_y:2 + step_y + columns]

    centre = beside(u, 0, 0)
    act = 0.5 * growth(u)
    spread = sum((beside(act, 0, 0) + beside(act, *s)) * (beside(u, *s) - centre) for s in ((1, 0), (-1, 0), (0, 1), (0, -1)))
    near_x, far_x = (jnp.where(sign_x > 0, beside(u, -k, 0), beside(u, k, 0)) for k in (1, 2))
    near_y, far_y = (jnp.where(sign_y > 0, beside(u, 0, -k), beside(u, 0, k)) for k in (1, 2))
    carried = wind[0] * (3.0 * centre - 4.0 * near_x + far_x) + wind[1] * (3.0 * centre - 4.0 * near_y + far_y)
    below = jnp.concatenate([centre[:, :, :1], centre[:, :, :-1]], axis=2)
    above = jnp.concatenate([centre[:, :, 1:], centre[:, :, -1:]], axis=2)
    return strength * spread - 0.5 * carried + mixing * (below + above - 2.0 * centre)


def slice_shards(state, code, wind, mixing, sizes):
    word = code[0, 0]
    strength = jnp.where(word // 4 == 1, diffusion_high, diffusion_low)

    def rate_of(u):
        return tendency(padded(u, (("gx", 0), ("gy", 1)), 2), 1 - 2 * (word % 2), 1 - 2 * (word // 2 % 2), strength, wind, mixing)

    start_rate = rate_of(state)
    last, rates = state, (start_rate,) * 3
    for _ in range(SWEEPS):
        arrived = lax.ppermute((last, rates[2]), "tm", [(i, i + 1) for i in range(sizes[0] - 1)])
        first, g0 = (jnp.where(lax.axis_index("tm") == 0, a, b) for a, b in zip((state, start_rate), arrived))
        middle = first + half_step * (g0 - rates[0]) + time_step * sum(w * r for w, r in zip(first_weights, rates))
        g1 = rate_of(middle)
        last = middle + half_step * (g1 - rates[1]) + time_step * sum(w * r for w, r in zip(second_weights, rates))
        rates = g0, g1, rate_of(last)
    return middle[None], last[None]


def solution(mesh):
    sizes = tuple(mesh.shape[a] for a in ("tm", "gx", "gy"))
    run = pair_shards if sizes[0] == 2 else slice_shards

    def shards(start_states, wind_code, wind_profile, vertical_mix):
        return run(start_states[0], wind_code, wind_profile, vertical_mix, sizes)

    in_specs = (P("tm", "gx", "gy", None), P("gx", "gy"), P(), P("gx", "gy", None))
    out_specs = (P("tm", "gx", "gy", None), P("tm", "gx", "gy", None))
    return jax.shard_map(shards, mesh=mesh, in_specs=in_specs, out_specs=out_specs, check_vma=False)
```

```python
import functools
import jax
import jax.numpy as jnp
from jax import lax
from jax.experimental import pallas as pl
from jax.experimental.pallas import tpu as pltpu
from jax.sharding import PartitionSpec as P

SWEEPS = 3
HALO = 4 * SWEEPS
LANES = 128
TILE = 8
time_step = 0.5
half_step = 0.25
diffusion_low = 0.04
diffusion_high = 0.1
first_weights = (5.0 / 24.0, 1.0 / 3.0, -1.0 / 24.0)
second_weights = (-1.0 / 24.0, 1.0 / 3.0, 5.0 / 24.0)


def row_classes(reach, own):
    steps = reach // 2
    groups = {}
    for a in range(steps + 1):
        beside = 2 * (steps - a) if a else reach
        groups.setdefault((-(-(own + 2 * beside) // TILE), a == 0), []).append((a, beside))
    out = []
    for (tiles, _), members in sorted(groups.items()):
        beside = max(b for _, b in members)
        begins = range(max(2, HALO + own + beside - TILE * tiles), HALO - beside + 1)
        cuts = lambda begin: sum(begin < e < begin + TILE * tiles and (e - begin) % TILE > 0 for e in (HALO, HALO + own))
        out.append((tiles, min(begins, key=cuts), members[0][0], members[-1][0]))
    return out


def growth(u):
    return 1.5 - 1.0 / (1.0 + u * u)


def sweeps(stages, part, own_rows, own_columns, codes, wind, mix, start, mid, last_1, last_2, f, g1, g1b, g2, g2b,
           act_a, act_b, write):
    halves = mix.shape[0]
    slices, parts = range(start.shape[0]), range(halves)
    scale = 0.5 * half_step
    lane = lax.broadcasted_iota(jnp.int32, (TILE, LANES), 1)
    line = lax.broadcasted_iota(jnp.int32, (TILE, LANES), 0)
    bottom, top = lane == 0, lane == LANES - 1
    cx = [jnp.broadcast_to(-0.5 * half_step * wind[0:1, z * LANES:(z + 1) * LANES], (TILE, LANES)) for z in parts]
    cy = [jnp.broadcast_to(-0.5 * half_step * wind[1:2, z * LANES:(z + 1) * LANES], (TILE, LANES)) for z in parts]
    c3 = [3.0 * (a + b) for a, b in zip(cx, cy)]

    def merge(edges, values):
        got = values[-1]
        for e, value in zip(reversed(edges), reversed(values[:-1])):
            got = jnp.where(line < e, value, got)
        return got

    def evaluate(reach, source, active, finish):
        def block(x, count, column, tiles):
            rows = range(count)
            puts, below_flux = [], {}
            for k in range(tiles):
                y = column + TILE * k
                edges = [e - y for e in (HALO, HALO + own_columns) if y < e < y + TILE]
                sides = [sum(p >= e for e in (HALO, HALO + own_columns)) for p in [y] + [y + e for e in edges]]
                words = [codes[x * 3 + j] for j in sides]
                kh = [jnp.where(w >= 8, 0.0, jnp.where(w >= 4, scale * diffusion_high, scale * diffusion_low)) for w in words]
                step_x = [1 - 2 * (w & 1) for w in words]
                step_y = [1 - (w & 2) for w in words]
                strength = merge(edges, [jnp.full((TILE, LANES), s, jnp.float32) for s in kh])
                rates = {}
                for n in slices:
                    def u_at(z, i, j):
                        return source[n, z, x + i, pl.ds(y + j, TILE), :]

                    def a_at(z, i, j):
                        return active[n, z, x + i, pl.ds(y + j, TILE), :]

                    centre = {(z, r): u_at(z, r, 0) for z in parts for r in rows}
                    ups = {c: pltpu.roll(u, LANES - 1, 1) for c, u in centre.items()}
                    downs = {c: pltpu.roll(u, 1, 1) for c, u in centre.items()}
                    total = {}
                    for z in parts:
                        col = [u_at(z, -1, 0)] + [centre[z, r] for r in rows] + [u_at(z, count, 0)]
                        act = [a_at(z, i, 0) for i in range(-1, count + 1)]
                        flux = [(act[i] + act[i + 1]) * (col[i + 1] - col[i]) for i in range(count + 1)]
                        for r in rows:
                            uc, ac = col[r + 1], act[r + 1]
                            up = (ac + a_at(z, r, 1)) * (u_at(z, r, 1) - uc)
                            moved = pltpu.roll(up, 1, 0)
                            if k:
                                down = jnp.where(line == 0, below_flux[n, z, r], moved)
                            else:
                                down = (ac + a_at(z, r, -1)) * (uc - u_at(z, r, -1))
                            below_flux[n, z, r] = moved
                            spread = (flux[r + 1] - flux[r]) + (up - down)
                            near_x = merge(edges, [u_at(z, r - s, 0) for s in step_x])
                            far_x = merge(edges, [u_at(z, r - 2 * s, 0) for s in step_x])
                            near_y = merge(edges, [u_at(z, r, -s) for s in step_y])
                            far_y = merge(edges, [u_at(z, r, -2 * s) for s in step_y])
                            total[z, r] = ((strength * spread + c3[z] * uc) + cx[z] * (far_x - 4.0 * near_x)
                                           + cy[z] * (far_y - 4.0 * near_y))
                    for r in rows:
                        for z in parts:
                            u = centre[z, r]
                            above = jnp.where(top, ups[z + 1, r] if z + 1 < halves else u, ups[z, r])
                            below = jnp.where(bottom, downs[z - 1, r] if z else u, downs[z, r])
                            bend = (above - u) + (below - u)
                            rate = total[z, r] + mix[z, x + r, pl.ds(y, TILE), :] * bend
                            rates[n, z, r] = rate

                            def get(ref, m=n):
                                return ref[m, z, x + r, pl.ds(y, TILE), :]

                            def put(ref, value):
                                puts.append((ref, (n, z, x + r, y), value))
                            finish(get, put, n, rates.get((n - 1, z, r), rate), u, rate)
            for ref, at, value in puts:
                write(ref, at, value)

        for tiles, column, near, far in row_classes(reach, own_columns):
            column, tiles = part(column, tiles)
            if near == 0:
                group = 4 if own_rows % 4 == 0 else 2

                @pl.loop(0, own_rows // group)
                def _(i, column=column, tiles=tiles, group=group):
                    block(HALO + group * i, group, column, tiles)
            else:
                span = 2 * (far - near + 1)
                group = 4 if span % 4 == 0 else 2
                width = span // group

                @pl.loop(0, 2 * width, unroll=2 if group == 2 else 1)
                def _(i, column=column, tiles=tiles, near=near, far=far, width=width, group=group):
                    low = HALO - 2 * far + group * i
                    high = HALO + own_rows + 2 * (near - 1) + group * (i - width)
                    block(jnp.where(i < width, low, high), group, column, tiles)

    w1 = [time_step / half_step * w for w in first_weights]
    w2 = [time_step / half_step * w for w in second_weights]
    assert abs(sum(w1) - 1) < 1e-12 and abs(sum(w2) - 1) < 1e-12

    def end_1(get, put, n, earlier, u, rate):
        m = get(start, max(n - 1, 0)) + ((earlier - rate) + rate)
        put(f, rate)
        put(mid, m)
        put(act_b, growth(m))

    def end_2(get, put, n, earlier, u, rate):
        first = get(f)
        last = u + ((rate - first) + first)
        put(g1, rate)
        put(last_1, last)
        put(act_a, growth(last))

    def end_3(get, put, n, earlier, u, rate):
        begin = get(last_1, n - 1) if n else get(start, 0)
        g0 = earlier if n else get(f, 0)
        m = begin + g0 + (w1[0] - 1.0) * get(f, max(n - 1, 0)) + w1[1] * get(g1) + w1[2] * rate
        put(g2, rate)
        put(mid, m)
        put(act_b, growth(m))

    def end_4(get, put, n, earlier, u, rate):
        last = u + rate + w2[0] * get(f, max(n - 1, 0)) + (w2[1] - 1.0) * get(g1) + w2[2] * get(g2)
        put(g1b, rate)
        put(last_2, last)
        put(act_a, growth(last))

    def end_5(get, put, n, earlier, u, rate):
        begin = get(last_2, n - 1) if n else get(start, 0)
        g0 = earlier if n else get(f, 0)
        before = get(g2, n - 1) if n else get(f, 0)
        m = begin + g0 + (w1[0] - 1.0) * before + w1[1] * get(g1b) + w1[2] * rate
        put(g2b, rate)
        put(mid, m)
        put(act_b, growth(m))

    def end_6(get, put, n, earlier, u, rate):
        before = get(g2, n - 1) if n else get(f, 0)
        put("middle", u)
        put("final", u + rate + w2[0] * before + (w2[1] - 1.0) * get(g1b) + w2[2] * get(g2b))

    every = ((10, start, act_a, end_1), (8, mid, act_b, end_2), (6, last_1, act_a, end_3),
             (4, mid, act_b, end_4), (2, last_2, act_a, end_5), (0, mid, act_b, end_6))
    for stage in stages:
        evaluate(*every[stage])


def whole(column, tiles):
    return column, tiles


def apart(low, own_columns, passed):
    def part(column, tiles):
        end = HALO + own_columns
        if low:
            free = sum(column + TILE * k + TILE + 2 <= end for k in range(tiles))
            return (column + TILE * free, tiles - free) if passed else (column, free)
        bound = sum(column + TILE * k - 2 < HALO for k in range(tiles))
        return (column, bound) if passed else (column + TILE * bound, tiles - bound)
    return part


def outside(word, low_x, low_y):
    return jnp.where(word == 0, 8 + (0 if low_x else 1) + (0 if low_y else 2), word - 1)


DEPTHS = (HALO, HALO, HALO - 2)


def corner_rows():
    out, offset = [], 0
    for a, depth in enumerate(DEPTHS):
        for d in range(depth - 2):
            wide = depth - 2 * (d // 2 + 1)
            out.append((a, d, offset, wide))
            offset += wide
    return out, offset


CORNER_ROWS, CORNER_SIZE = corner_rows()
BEFORE = tuple(sum(DEPTHS[:a]) for a in range(len(DEPTHS) + 1))


def load_kernel(*refs):
    made = [pltpu.make_async_copy(a, b, refs[6].at[k]) for k, (a, b) in enumerate(zip(refs[:3], refs[3:6]))]
    for one in made:
        one.start()
    for one in made:
        one.wait()


def pack_kernel(where_ref, code, own, other, mixing, beside_x, beside_y, diagonal_1, diagonal_2):
    t = where_ref[0]
    rows, columns, levels = own.shape
    word = jnp.full((TILE, LANES), (code[0, 0] + 1).astype(jnp.float32))
    for ref in (beside_x, beside_y, diagonal_1, diagonal_2):
        ref[0, pl.ds(ref.shape[1] - TILE, TILE), :] = word

    def side(low):
        arrays = (own, other, mixing) if low else (other, own, mixing)
        for z in range(levels // LANES):
            lanes = pl.ds(z * LANES, LANES)
            for a, depth in enumerate(DEPTHS):
                for i in range(depth):
                    x = i if low else rows - depth + i
                    beside_x[z, pl.ds((BEFORE[a] + i) * columns, columns), :] = arrays[a][x, :, lanes]
            for a, d, offset, wide in CORNER_ROWS:
                x = d if low else rows - 1 - d
                near, far = arrays[a][x, pl.ds(0, wide), lanes], arrays[a][x, pl.ds(columns - wide, wide), lanes]
                diagonal_1[z, pl.ds(offset, wide), :] = near if low else far
                diagonal_2[z, pl.ds(offset, wide), :] = far if low else near

        @pl.loop(0, rows // 2)
        def _(i):
            for x in (2 * i, 2 * i + 1):
                for z in range(levels // LANES):
                    for a, depth in enumerate(DEPTHS):
                        line = arrays[a][x, pl.ds(0 if low else columns - depth, depth), pl.ds(z * LANES, LANES)]
                        beside_y[z, pl.ds(BEFORE[a] * rows + x * depth, depth), :] = line

    pl.when(t == 0)(lambda: side(True))
    pl.when(t != 0)(lambda: side(False))


def filler(start, act, mix):
    def fill(a, z, x, y, value):
        at = (z, x, pl.ds(y, value.shape[0]), slice(None))
        if a < 2:
            start[(a, *at)] = value
            act[(a, *at)] = growth(value)
        else:
            mix[at] = half_step * value
    return fill


def fill_y(fill, arrived, low, beyond, own_shape):
    block_rows, columns, levels = own_shape
    inner = block_rows // 2 + HALO
    at_own, from_own = (HALO, 0) if low else (0, block_rows - inner)

    @pl.loop(0, inner // 4)
    def _(group):
        for r in range(4):
            i = 4 * group + r
            for z in range(levels // LANES):
                for a, depth in enumerate(DEPTHS):
                    value = arrived[z, pl.ds(BEFORE[a] * block_rows + (from_own + i) * depth, depth), :]
                    fill(a, z, at_own + i, HALO + columns if beyond else HALO - depth, value)


def fill_codes(low, code, words, codes, inner):
    word_x, word_y, word_p, word_1, word_2 = words
    at_own, at_x = (HALO, 0) if low else (0, inner)
    word_low, word_high = (word_y, word_p) if low else (word_p, word_y)
    corner_low, corner_high = (word_1, word_2) if low else (word_2, word_1)

    @pl.loop(0, inner)
    def _(i):
        codes[(at_own + i) * 3] = outside(word_low, True, True)
        codes[(at_own + i) * 3 + 1] = code[0, 0]
        codes[(at_own + i) * 3 + 2] = outside(word_high, True, False)

    @pl.loop(0, HALO)
    def _(i):
        codes[(at_x + i) * 3] = outside(corner_low, low, True)
        codes[(at_x + i) * 3 + 1] = outside(word_x, low, True)
        codes[(at_x + i) * 3 + 2] = outside(corner_high, low, False)


def word_of(ref):
    return jnp.max(ref[0, pl.ds(ref.shape[1] - TILE, TILE), :]).astype(jnp.int32)


def store(ref, at, value):
    n, z, x, y = at
    ref[n, z, x, pl.ds(y, TILE), :] = value


def fill_kernel(where_ref, code, wind, own, other, mixing, halo_x, halo_y, corner_1, corner_2,
                start, act_a, mix, f, mid, act_b, codes):
    t = where_ref[0]
    block_rows, columns, levels = own.shape
    halves = levels // LANES
    inner = block_rows // 2 + HALO
    fill = filler(start, act_a, mix)
    words = [word_of(halo_x), word_of(halo_y), 0, word_of(corner_1), word_of(corner_2)]

    def side(low):
        at_own, from_own = (HALO, 0) if low else (0, block_rows - inner)
        low_corner, high_corner = (corner_1, corner_2) if low else (corner_2, corner_1)
        arrays = (own, other, mixing) if low else (other, own, mixing)
        fill_codes(low, code, words, codes, inner)

        @pl.loop(0, inner // 4)
        def _(group):
            for r in range(4):
                i = 4 * group + r
                for z in range(halves):
                    for a in range(len(DEPTHS)):
                        for y in range(0, columns, TILE):
                            fill(a, z, at_own + i, HALO + y, arrays[a][from_own + i, pl.ds(y, TILE), pl.ds(z * LANES, LANES)])

        fill_y(fill, halo_y, low, not low, own.shape)
        for z in range(halves):
            for a, depth in enumerate(DEPTHS):
                for i in range(depth):
                    x = HALO - depth + i if low else inner + i
                    for y in range(0, columns, TILE):
                        fill(a, z, x, HALO + y, halo_x[z, pl.ds((BEFORE[a] + i) * columns + y, TILE), :])
            for a, d, offset, wide in CORNER_ROWS:
                x = HALO - 1 - d if low else inner + d
                fill(a, z, x, HALO - wide, low_corner[z, pl.ds(offset, wide), :])
                fill(a, z, x, HALO + columns, high_corner[z, pl.ds(offset, wide), :])
        sweeps((0,), apart(low, columns, False), block_rows // 2, columns, codes, wind, mix, start, mid, None, None, f,
               None, None, None, None, act_a, act_b, store)

    pl.when(t == 0)(lambda: side(True))
    pl.when(t != 0)(lambda: side(False))


def pair_kernel(where_ref, code, wind, halo_x, halo_y, passed_y, corner_1, corner_2, *rest):
    mine, theirs, start, act_a, mix, f, mid, act_b, last_1, last_2, g1, g1b, g2, g2b, both, codes = rest[6:]
    t = where_ref[0]
    half, columns = both.shape[2:4]
    words = [word_of(r) for r in (halo_x, halo_y, passed_y, corner_1, corner_2)]

    def run(stages, part, write):
        sweeps(stages, part, half, columns, codes, wind, mix, start, mid, last_1, last_2, f, g1, g1b, g2, g2b, act_a, act_b, write)

    def side(low):
        fill_codes(low, code, words, codes, half + HALO)
        fill_y(filler(start, act_a, mix), passed_y, low, low, (2 * half, columns, both.shape[4]))
        run((0,), apart(low, columns, True), store)

    pl.when(t == 0)(lambda: side(True))
    pl.when(t != 0)(lambda: side(False))

    def write(ref, at, value):
        n, z, x, y = at
        if isinstance(ref, str):
            place = jnp.where(t == n, 0, 1)
            both[place, 0 if ref == "middle" else 1, x - HALO, pl.ds(y - HALO, TILE), pl.ds(z * LANES, LANES)] = value
        else:
            store(ref, at, value)

    run(range(1, 6), whole, write)
    mine[...] = both[0]
    theirs[...] = both[1]


def merge_kernel(where_ref, mine, got, middle, final, semaphores):
    t = where_ref[0]
    half = mine.shape[1]

    def merge(low):
        halves = (mine, got) if low else (got, mine)
        made = [pltpu.make_async_copy(part.at[k], out.at[pl.ds(h * half, half)], semaphores.at[2 * h + k])
                for h, part in enumerate(halves) for k, out in enumerate((middle, final))]
        for one in made:
            one.start()
        for one in made:
            one.wait()

    pl.when(t == 0)(lambda: merge(True))
    pl.when(t != 0)(lambda: merge(False))


VMEM = pl.BlockSpec(memory_space=pltpu.VMEM)
SMEM = pl.BlockSpec(memory_space=pltpu.SMEM)
ANY = pl.BlockSpec(memory_space=pl.ANY)
LIMIT = 30 * 2**20


def of(*shape):
    return jax.ShapeDtypeStruct(shape, jnp.float32)


def near(x):
    return pltpu.with_memory_space_constraint(x, pltpu.VMEM)


def pair_shards(state, code, wind, mixing, sizes):
    axes = ("tm", "gx", "gy")
    rows, columns, levels = state.shape
    halves = levels // LANES
    t = lax.axis_index("tm")
    where = t.astype(jnp.int32).reshape(1)

    def partners(step_x, step_y):
        pairs = []
        for x in range(sizes[1]):
            for y in range(sizes[2]):
                u, v = x - step_x, y - step_y
                if 0 <= u < sizes[1] and 0 <= v < sizes[2]:
                    here, there = x * sizes[2] + y, (sizes[1] + u) * sizes[2] + v
                    pairs += [(here, there), (there, here)]
        return pairs

    swap = [(0, 1), (1, 0)]
    small = pltpu.CompilerParams(vmem_limit_bytes=4 * 2**20)
    other = near(lax.ppermute(state, "tm", swap))
    local = state, mixing, wind
    local = pl.pallas_call(
        load_kernel, out_shape=[pltpu.VMEM(x.shape, jnp.float32) for x in local],
        in_specs=[ANY] * 3, out_specs=[VMEM] * 3, scratch_shapes=[pltpu.SemaphoreType.DMA((3,))],
        compiler_params=pltpu.CompilerParams(vmem_limit_bytes=60 * 2**20),
        cost_estimate=pl.CostEstimate(flops=0, bytes_accessed=16 * state.size, transcendentals=0),
    )(*local)
    state, mixing, wind = map(near, local)
    corner = (halves, CORNER_SIZE + TILE, LANES)
    to_x, to_y, to_1, to_2 = pl.pallas_call(
        pack_kernel,
        out_shape=[pltpu.VMEM(s, jnp.float32) for s in (
            (halves, BEFORE[-1] * columns + TILE, LANES), (halves, BEFORE[-1] * rows + TILE, LANES), corner, corner)],
        in_specs=[SMEM, SMEM, VMEM, VMEM, VMEM], out_specs=[VMEM] * 4,
        compiler_params=small,
    )(where, code, state, other, mixing)
    halo_x = lax.ppermute(to_x, axes, partners(1, 0))
    halo_y = lax.ppermute(to_y, axes, partners(0, 1))
    corner_1 = lax.ppermute(to_1, axes, partners(1, 1))
    corner_2 = lax.ppermute(to_2, axes, partners(1, -1))
    halo_x, halo_y, corner_1, corner_2 = lax.optimization_barrier((halo_x, halo_y, corner_1, corner_2))
    passed_y = near(lax.ppermute(halo_y, "tm", swap))
    halo_x, halo_y, corner_1, corner_2 = map(near, (halo_x, halo_y, corner_1, corner_2))
    half = rows // 2
    plane = (halves, half + 2 * HALO, columns + 2 * HALO + TILE, LANES)
    planes = [pltpu.VMEM(s, jnp.float32) for s in ((2, *plane), (2, *plane), plane, (2, *plane), (2, *plane), (2, *plane))]
    params = pltpu.CompilerParams(vmem_limit_bytes=LIMIT)
    filled = pl.pallas_call(
        fill_kernel, out_shape=planes, in_specs=[SMEM, SMEM] + [VMEM] * 8, out_specs=[VMEM] * 6,
        scratch_shapes=[pltpu.SMEM((3 * (half + 2 * HALO),), jnp.int32)], compiler_params=small,
        cost_estimate=pl.CostEstimate(flops=0, bytes_accessed=1 << 23, transcendentals=0),
    )(where, code, wind, state, other, mixing, halo_x, halo_y, corner_1, corner_2)
    mine, theirs, *_ = pl.pallas_call(
        pair_kernel, out_shape=[pltpu.VMEM((2, half, columns, levels), jnp.float32)] * 2 + planes,
        in_specs=[SMEM, SMEM] + [VMEM] * 12, out_specs=[VMEM] * 8, input_output_aliases={8 + k: 2 + k for k in range(6)},
        scratch_shapes=[pltpu.VMEM((2, *plane), jnp.float32)] * 6 + [
            pltpu.VMEM((2, 2, half, columns, levels), jnp.float32), pltpu.SMEM((3 * (half + 2 * HALO),), jnp.int32)],
        compiler_params=params,
    )(where, code, wind, halo_x, halo_y, passed_y, corner_1, corner_2, *map(near, filled))
    got = lax.ppermute(theirs, "tm", swap)
    middle, final = pl.pallas_call(
        merge_kernel, out_shape=[of(*state.shape)] * 2, in_specs=[SMEM, VMEM, VMEM], out_specs=[ANY] * 2,
        scratch_shapes=[pltpu.SemaphoreType.DMA((4,))], compiler_params=small,
    )(where, near(mine), near(got))
    return middle[None], final[None]


def padded(x, sides, width):
    for axis, dim in sides:
        devices, length = lax.axis_size(axis), x.shape[dim]
        up = [(i, i + 1) for i in range(devices - 1)]
        down = [(j, i) for i, j in up]
        before = lax.ppermute(lax.slice_in_dim(x, length - width, length, axis=dim), axis, up)
        after = lax.ppermute(lax.slice_in_dim(x, 0, width, axis=dim), axis, down)
        x = jnp.concatenate([before, x, after], axis=dim)
    return x


def tendency(u, sign_x, sign_y, strength, wind, mixing):
    rows, columns = mixing.shape[:2]

    def beside(source, step_x, step_y):
        return source[2 + step_x:2 + step_x + rows, 2 + step_y:2 + step_y + columns]

    centre = beside(u, 0, 0)
    act = 0.5 * growth(u)
    spread = sum((beside(act, 0, 0) + beside(act, *s)) * (beside(u, *s) - centre) for s in ((1, 0), (-1, 0), (0, 1), (0, -1)))
    near_x, far_x = (jnp.where(sign_x > 0, beside(u, -k, 0), beside(u, k, 0)) for k in (1, 2))
    near_y, far_y = (jnp.where(sign_y > 0, beside(u, 0, -k), beside(u, 0, k)) for k in (1, 2))
    carried = wind[0] * (3.0 * centre - 4.0 * near_x + far_x) + wind[1] * (3.0 * centre - 4.0 * near_y + far_y)
    below = jnp.concatenate([centre[:, :, :1], centre[:, :, :-1]], axis=2)
    above = jnp.concatenate([centre[:, :, 1:], centre[:, :, -1:]], axis=2)
    return strength * spread - 0.5 * carried + mixing * (below + above - 2.0 * centre)


def slice_shards(state, code, wind, mixing, sizes):
    word = code[0, 0]
    strength = jnp.where(word // 4 == 1, diffusion_high, diffusion_low)

    def rate_of(u):
        return tendency(padded(u, (("gx", 0), ("gy", 1)), 2), 1 - 2 * (word % 2), 1 - 2 * (word // 2 % 2), strength, wind, mixing)

    start_rate = rate_of(state)
    last, rates = state, (start_rate,) * 3
    for _ in range(SWEEPS):
        arrived = lax.ppermute((last, rates[2]), "tm", [(i, i + 1) for i in range(sizes[0] - 1)])
        first, g0 = (jnp.where(lax.axis_index("tm") == 0, a, b) for a, b in zip((state, start_rate), arrived))
        middle = first + half_step * (g0 - rates[0]) + time_step * sum(w * r for w, r in zip(first_weights, rates))
        g1 = rate_of(middle)
        last = middle + half_step * (g1 - rates[1]) + time_step * sum(w * r for w, r in zip(second_weights, rates))
        rates = g0, g1, rate_of(last)
    return middle[None], last[None]


def solution(mesh):
    sizes = tuple(mesh.shape[a] for a in ("tm", "gx", "gy"))
    run = pair_shards if sizes[0] == 2 else slice_shards

    def shards(start_states, wind_code, wind_profile, vertical_mix):
        return run(start_states[0], wind_code, wind_profile, vertical_mix, sizes)

    in_specs = (P("tm", "gx", "gy", None), P("gx", "gy"), P(), P("gx", "gy", None))
    out_specs = (P("tm", "gx", "gy", None), P("tm", "gx", "gy", None))
    return jax.shard_map(shards, mesh=mesh, in_specs=in_specs, out_specs=out_specs, check_vma=False)
```

```python
import functools
import jax
import jax.numpy as jnp
from jax import lax
from jax.experimental import pallas as pl
from jax.experimental.pallas import tpu as pltpu
from jax.sharding import PartitionSpec as P

SWEEPS = 3
HALO = 4 * SWEEPS
LANES = 128
TILE = 8
time_step = 0.5
half_step = 0.25
diffusion_low = 0.04
diffusion_high = 0.1
first_weights = (5.0 / 24.0, 1.0 / 3.0, -1.0 / 24.0)
second_weights = (-1.0 / 24.0, 1.0 / 3.0, 5.0 / 24.0)


def row_classes(reach, own):
    steps = reach // 2
    groups = {}
    for a in range(steps + 1):
        beside = 2 * (steps - a) if a else reach
        groups.setdefault((-(-(own + 2 * beside) // TILE), a == 0), []).append((a, beside))
    out = []
    for (tiles, _), members in sorted(groups.items()):
        beside = max(b for _, b in members)
        begins = range(max(2, HALO + own + beside - TILE * tiles), HALO - beside + 1)
        cuts = lambda begin: sum(begin < e < begin + TILE * tiles and (e - begin) % TILE > 0 for e in (HALO, HALO + own))
        out.append((tiles, min(begins, key=cuts), members[0][0], members[-1][0]))
    return out


def growth(u):
    return 1.5 - 1.0 / (1.0 + u * u)


def sweeps(stages, part, own_rows, own_columns, codes, wind, mix, start, mid, last_1, last_2, f, g1, g1b, g2, g2b,
           act_a, act_b, write):
    halves = mix.shape[0]
    slices, parts = range(start.shape[0]), range(halves)
    scale = 0.5 * half_step
    lane = lax.broadcasted_iota(jnp.int32, (TILE, LANES), 1)
    line = lax.broadcasted_iota(jnp.int32, (TILE, LANES), 0)
    bottom, top = lane == 0, lane == LANES - 1
    cx = [jnp.broadcast_to(-0.5 * half_step * wind[0:1, z * LANES:(z + 1) * LANES], (TILE, LANES)) for z in parts]
    cy = [jnp.broadcast_to(-0.5 * half_step * wind[1:2, z * LANES:(z + 1) * LANES], (TILE, LANES)) for z in parts]
    c3 = [3.0 * (a + b) for a, b in zip(cx, cy)]

    def merge(edges, values):
        got = values[-1]
        for e, value in zip(reversed(edges), reversed(values[:-1])):
            got = jnp.where(line < e, value, got)
        return got

    def evaluate(reach, source, active, finish):
        def block(x, count, column, tiles):
            rows = range(count)
            puts, below_flux = [], {}
            for k in range(tiles):
                y = column + TILE * k
                edges = [e - y for e in (HALO, HALO + own_columns) if y < e < y + TILE]
                sides = [sum(p >= e for e in (HALO, HALO + own_columns)) for p in [y] + [y + e for e in edges]]
                words = [codes[x * 3 + j] for j in sides]
                kh = [jnp.where(w >= 8, 0.0, jnp.where(w >= 4, scale * diffusion_high, scale * diffusion_low)) for w in words]
                step_x = [1 - 2 * (w & 1) for w in words]
                step_y = [1 - (w & 2) for w in words]
                strength = merge(edges, [jnp.full((TILE, LANES), s, jnp.float32) for s in kh])
                rates = {}
                for n in slices:
                    def u_at(z, i, j):
                        return source[n, z, x + i, pl.ds(y + j, TILE), :]

                    def a_at(z, i, j):
                        return active[n, z, x + i, pl.ds(y + j, TILE), :]

                    centre = {(z, r): u_at(z, r, 0) for z in parts for r in rows}
                    ups = {c: pltpu.roll(u, LANES - 1, 1) for c, u in centre.items()}
                    downs = {c: pltpu.roll(u, 1, 1) for c, u in centre.items()}
                    total = {}
                    for z in parts:
                        col = [u_at(z, -1, 0)] + [centre[z, r] for r in rows] + [u_at(z, count, 0)]
                        act = [a_at(z, i, 0) for i in range(-1, count + 1)]
                        flux = [(act[i] + act[i + 1]) * (col[i + 1] - col[i]) for i in range(count + 1)]
                        for r in rows:
                            uc, ac = col[r + 1], act[r + 1]
                            up = (ac + a_at(z, r, 1)) * (u_at(z, r, 1) - uc)
                            moved = pltpu.roll(up, 1, 0)
                            if k:
                                down = jnp.where(line == 0, below_flux[n, z, r], moved)
                            else:
                                down = (ac + a_at(z, r, -1)) * (uc - u_at(z, r, -1))
                            below_flux[n, z, r] = moved
                            spread = (flux[r + 1] - flux[r]) + (up - down)
                            near_x = merge(edges, [u_at(z, r - s, 0) for s in step_x])
                            far_x = merge(edges, [u_at(z, r - 2 * s, 0) for s in step_x])
                            near_y = merge(edges, [u_at(z, r, -s) for s in step_y])
                            far_y = merge(edges, [u_at(z, r, -2 * s) for s in step_y])
                            total[z, r] = ((strength * spread + c3[z] * uc) + cx[z] * (far_x - 4.0 * near_x)
                                           + cy[z] * (far_y - 4.0 * near_y))
                    for r in rows:
                        for z in parts:
                            u = centre[z, r]
                            above = jnp.where(top, ups[z + 1, r] if z + 1 < halves else u, ups[z, r])
                            below = jnp.where(bottom, downs[z - 1, r] if z else u, downs[z, r])
                            bend = (above - u) + (below - u)
                            rate = total[z, r] + mix[z, x + r, pl.ds(y, TILE), :] * bend
                            rates[n, z, r] = rate

                            def get(ref, m=n):
                                return ref[m, z, x + r, pl.ds(y, TILE), :]

                            def put(ref, value):
                                puts.append((ref, (n, z, x + r, y), value))
                            finish(get, put, n, rates.get((n - 1, z, r), rate), u, rate)
            for ref, at, value in puts:
                write(ref, at, value)

        for tiles, column, near, far in row_classes(reach, own_columns):
            column, tiles = part(column, tiles)
            if near == 0:
                group = 4 if own_rows % 4 == 0 else 2

                @pl.loop(0, own_rows // group, unroll=2)
                def _(i, column=column, tiles=tiles, group=group):
                    block(HALO + group * i, group, column, tiles)
            else:
                span = 2 * (far - near + 1)
                group = 4 if span % 4 == 0 else 2
                width = span // group

                @pl.loop(0, 2 * width, unroll=2 if group == 2 else 1)
                def _(i, column=column, tiles=tiles, near=near, far=far, width=width, group=group):
                    low = HALO - 2 * far + group * i
                    high = HALO + own_rows + 2 * (near - 1) + group * (i - width)
                    block(jnp.where(i < width, low, high), group, column, tiles)

    w1 = [time_step / half_step * w for w in first_weights]
    w2 = [time_step / half_step * w for w in second_weights]
    assert abs(sum(w1) - 1) < 1e-12 and abs(sum(w2) - 1) < 1e-12

    def end_1(get, put, n, earlier, u, rate):
        m = get(start, max(n - 1, 0)) + ((earlier - rate) + rate)
        put(f, rate)
        put(mid, m)
        put(act_b, growth(m))

    def end_2(get, put, n, earlier, u, rate):
        first = get(f)
        last = u + ((rate - first) + first)
        put(g1, rate)
        put(last_1, last)
        put(act_a, growth(last))

    def end_3(get, put, n, earlier, u, rate):
        begin = get(last_1, n - 1) if n else get(start, 0)
        g0 = earlier if n else get(f, 0)
        m = begin + g0 + (w1[0] - 1.0) * get(f, max(n - 1, 0)) + w1[1] * get(g1) + w1[2] * rate
        put(g2, rate)
        put(mid, m)
        put(act_b, growth(m))

    def end_4(get, put, n, earlier, u, rate):
        last = u + rate + w2[0] * get(f, max(n - 1, 0)) + (w2[1] - 1.0) * get(g1) + w2[2] * get(g2)
        put(g1b, rate)
        put(last_2, last)
        put(act_a, growth(last))

    def end_5(get, put, n, earlier, u, rate):
        begin = get(last_2, n - 1) if n else get(start, 0)
        g0 = earlier if n else get(f, 0)
        before = get(g2, n - 1) if n else get(f, 0)
        m = begin + g0 + (w1[0] - 1.0) * before + w1[1] * get(g1b) + w1[2] * rate
        put(g2b, rate)
        put(mid, m)
        put(act_b, growth(m))

    def end_6(get, put, n, earlier, u, rate):
        before = get(g2, n - 1) if n else get(f, 0)
        put("middle", u)
        put("final", u + rate + w2[0] * before + (w2[1] - 1.0) * get(g1b) + w2[2] * get(g2b))

    every = ((10, start, act_a, end_1), (8, mid, act_b, end_2), (6, last_1, act_a, end_3),
             (4, mid, act_b, end_4), (2, last_2, act_a, end_5), (0, mid, act_b, end_6))
    for stage in stages:
        evaluate(*every[stage])


def whole(column, tiles):
    return column, tiles


def apart(low, own_columns, passed):
    def part(column, tiles):
        end = HALO + own_columns
        if low:
            free = sum(column + TILE * k + TILE + 2 <= end for k in range(tiles))
            return (column + TILE * free, tiles - free) if passed else (column, free)
        bound = sum(column + TILE * k - 2 < HALO for k in range(tiles))
        return (column, bound) if passed else (column + TILE * bound, tiles - bound)
    return part


def outside(word, low_x, low_y):
    return jnp.where(word == 0, 8 + (0 if low_x else 1) + (0 if low_y else 2), word - 1)


DEPTHS = (HALO, HALO, HALO - 2)


def corner_rows():
    out, offset = [], 0
    for a, depth in enumerate(DEPTHS):
        for d in range(depth - 2):
            wide = depth - 2 * (d // 2 + 1)
            out.append((a, d, offset, wide))
            offset += wide
    return out, offset


CORNER_ROWS, CORNER_SIZE = corner_rows()
BEFORE = tuple(sum(DEPTHS[:a]) for a in range(len(DEPTHS) + 1))


def load_kernel(*refs):
    made = [pltpu.make_async_copy(a, b, refs[6].at[k]) for k, (a, b) in enumerate(zip(refs[:3], refs[3:6]))]
    for one in made:
        one.start()
    for one in made:
        one.wait()


def pack_kernel(where_ref, code, own, other, mixing, beside_x, diagonal_1, diagonal_2, *beside_y):
    t = where_ref[0]
    rows, columns, levels = own.shape
    word = jnp.full((TILE, LANES), (code[0, 0] + 1).astype(jnp.float32))
    for ref in (beside_x, diagonal_1, diagonal_2, *beside_y):
        ref[0, pl.ds(ref.shape[1] - TILE, TILE), :] = word

    def side(low):
        arrays = (own, other, mixing) if low else (other, own, mixing)
        for z in range(levels // LANES):
            lanes = pl.ds(z * LANES, LANES)
            for a, depth in enumerate(DEPTHS):
                for i in range(depth):
                    x = i if low else rows - depth + i
                    beside_x[z, pl.ds((BEFORE[a] + i) * columns, columns), :] = arrays[a][x, :, lanes]
            for a, d, offset, wide in CORNER_ROWS:
                x = d if low else rows - 1 - d
                near, far = arrays[a][x, pl.ds(0, wide), lanes], arrays[a][x, pl.ds(columns - wide, wide), lanes]
                diagonal_1[z, pl.ds(offset, wide), :] = near if low else far
                diagonal_2[z, pl.ds(offset, wide), :] = far if low else near

        @pl.loop(0, rows // 2)
        def _(i):
            for x in (2 * i, 2 * i + 1):
                for z in range(levels // LANES):
                    for a, depth in enumerate(DEPTHS):
                        line = arrays[a][x, pl.ds(0 if low else columns - depth, depth), pl.ds(z * LANES, LANES)]
                        beside_y[z][0, pl.ds(BEFORE[a] * rows + x * depth, depth), :] = line

    pl.when(t == 0)(lambda: side(True))
    pl.when(t != 0)(lambda: side(False))


def filler(start, act, mix):
    def fill(a, z, x, y, value):
        at = (z, x, pl.ds(y, value.shape[0]), slice(None))
        if a < 2:
            start[(a, *at)] = value
            act[(a, *at)] = growth(value)
        else:
            mix[at] = half_step * value
    return fill


def fill_y(fill, arrived, low, beyond, own_shape):
    block_rows, columns, levels = own_shape
    inner = block_rows // 2 + HALO
    at_own, from_own = (HALO, 0) if low else (0, block_rows - inner)

    @pl.loop(0, inner // 4)
    def _(group):
        for r in range(4):
            i = 4 * group + r
            for z in range(levels // LANES):
                for a, depth in enumerate(DEPTHS):
                    value = arrived[z][0, pl.ds(BEFORE[a] * block_rows + (from_own + i) * depth, depth), :]
                    fill(a, z, at_own + i, HALO + columns if beyond else HALO - depth, value)


def fill_codes(low, code, words, codes, inner):
    word_x, word_y, word_p, word_1, word_2 = words
    at_own, at_x = (HALO, 0) if low else (0, inner)
    word_low, word_high = (word_y, word_p) if low else (word_p, word_y)
    corner_low, corner_high = (word_1, word_2) if low else (word_2, word_1)

    @pl.loop(0, inner)
    def _(i):
        codes[(at_own + i) * 3] = outside(word_low, True, True)
        codes[(at_own + i) * 3 + 1] = code[0, 0]
        codes[(at_own + i) * 3 + 2] = outside(word_high, True, False)

    @pl.loop(0, HALO)
    def _(i):
        codes[(at_x + i) * 3] = outside(corner_low, low, True)
        codes[(at_x + i) * 3 + 1] = outside(word_x, low, True)
        codes[(at_x + i) * 3 + 2] = outside(corner_high, low, False)


def word_of(ref):
    return jnp.max(ref[0, pl.ds(ref.shape[1] - TILE, TILE), :]).astype(jnp.int32)


def store(ref, at, value):
    n, z, x, y = at
    ref[n, z, x, pl.ds(y, TILE), :] = value


def fill_kernel(where_ref, code, wind, own, other, mixing, halo_x, corner_1, corner_2, *rest):
    t = where_ref[0]
    block_rows, columns, levels = own.shape
    halves = levels // LANES
    halo_y, (start, act_a, mix, f, mid, act_b, codes) = rest[:halves], rest[halves:]
    inner = block_rows // 2 + HALO
    fill = filler(start, act_a, mix)
    words = [word_of(halo_x), word_of(halo_y[0]), 0, word_of(corner_1), word_of(corner_2)]

    def side(low):
        at_own, from_own = (HALO, 0) if low else (0, block_rows - inner)
        low_corner, high_corner = (corner_1, corner_2) if low else (corner_2, corner_1)
        arrays = (own, other, mixing) if low else (other, own, mixing)
        fill_codes(low, code, words, codes, inner)

        @pl.loop(0, inner // 4)
        def _(group):
            for r in range(4):
                i = 4 * group + r
                for z in range(halves):
                    for a in range(len(DEPTHS)):
                        for y in range(0, columns, TILE):
                            fill(a, z, at_own + i, HALO + y, arrays[a][from_own + i, pl.ds(y, TILE), pl.ds(z * LANES, LANES)])

        fill_y(fill, halo_y, low, not low, own.shape)
        for z in range(halves):
            for a, depth in enumerate(DEPTHS):
                for i in range(depth):
                    x = HALO - depth + i if low else inner + i
                    for y in range(0, columns, TILE):
                        fill(a, z, x, HALO + y, halo_x[z, pl.ds((BEFORE[a] + i) * columns + y, TILE), :])
            for a, d, offset, wide in CORNER_ROWS:
                x = HALO - 1 - d if low else inner + d
                fill(a, z, x, HALO - wide, low_corner[z, pl.ds(offset, wide), :])
                fill(a, z, x, HALO + columns, high_corner[z, pl.ds(offset, wide), :])
        sweeps((0,), apart(low, columns, False), block_rows // 2, columns, codes, wind, mix, start, mid, None, None, f,
               None, None, None, None, act_a, act_b, store)

    pl.when(t == 0)(lambda: side(True))
    pl.when(t != 0)(lambda: side(False))


def pair_kernel(halves, where_ref, code, wind, halo_x, corner_1, corner_2, *rest):
    halo_y, passed_y = rest[:halves], rest[halves:2 * halves]
    mine, theirs, start, act_a, mix, f, mid, act_b, last_1, last_2, g1, g1b, g2, g2b, both, codes = rest[2 * halves + 6:]
    t = where_ref[0]
    half, columns = both.shape[2:4]
    words = [word_of(r) for r in (halo_x, halo_y[0], passed_y[0], corner_1, corner_2)]

    def run(stages, part, write):
        sweeps(stages, part, half, columns, codes, wind, mix, start, mid, last_1, last_2, f, g1, g1b, g2, g2b, act_a, act_b, write)

    def side(low):
        fill_codes(low, code, words, codes, half + HALO)
        fill_y(filler(start, act_a, mix), passed_y, low, low, (2 * half, columns, both.shape[4]))
        run((0,), apart(low, columns, True), store)

    pl.when(t == 0)(lambda: side(True))
    pl.when(t != 0)(lambda: side(False))

    def write(ref, at, value):
        n, z, x, y = at
        if isinstance(ref, str):
            place = jnp.where(t == n, 0, 1)
            both[place, 0 if ref == "middle" else 1, x - HALO, pl.ds(y - HALO, TILE), pl.ds(z * LANES, LANES)] = value
        else:
            store(ref, at, value)

    run(range(1, 6), whole, write)
    mine[...] = both[0]
    theirs[...] = both[1]


def merge_kernel(where_ref, mine, got, middle, final, semaphores):
    t = where_ref[0]
    half = mine.shape[1]

    def merge(low):
        halves = (mine, got) if low else (got, mine)
        made = [pltpu.make_async_copy(part.at[k], out.at[pl.ds(h * half, half)], semaphores.at[2 * h + k])
                for h, part in enumerate(halves) for k, out in enumerate((middle, final))]
        for one in made:
            one.start()
        for one in made:
            one.wait()

    pl.when(t == 0)(lambda: merge(True))
    pl.when(t != 0)(lambda: merge(False))


VMEM = pl.BlockSpec(memory_space=pltpu.VMEM)
SMEM = pl.BlockSpec(memory_space=pltpu.SMEM)
ANY = pl.BlockSpec(memory_space=pl.ANY)
LIMIT = 30 * 2**20


def of(*shape):
    return jax.ShapeDtypeStruct(shape, jnp.float32)


def near(x):
    return pltpu.with_memory_space_constraint(x, pltpu.VMEM)


def pair_shards(state, code, wind, mixing, sizes):
    axes = ("tm", "gx", "gy")
    rows, columns, levels = state.shape
    halves = levels // LANES
    t = lax.axis_index("tm")
    where = t.astype(jnp.int32).reshape(1)

    def partners(step_x, step_y):
        pairs = []
        for x in range(sizes[1]):
            for y in range(sizes[2]):
                u, v = x - step_x, y - step_y
                if 0 <= u < sizes[1] and 0 <= v < sizes[2]:
                    here, there = x * sizes[2] + y, (sizes[1] + u) * sizes[2] + v
                    pairs += [(here, there), (there, here)]
        return pairs

    swap = [(0, 1), (1, 0)]
    small = pltpu.CompilerParams(vmem_limit_bytes=4 * 2**20)
    other = near(lax.ppermute(state, "tm", swap))
    local = state, mixing, wind
    local = pl.pallas_call(
        load_kernel, out_shape=[pltpu.VMEM(x.shape, jnp.float32) for x in local],
        in_specs=[ANY] * 3, out_specs=[VMEM] * 3, scratch_shapes=[pltpu.SemaphoreType.DMA((3,))],
        compiler_params=pltpu.CompilerParams(vmem_limit_bytes=60 * 2**20),
        cost_estimate=pl.CostEstimate(flops=0, bytes_accessed=16 * state.size, transcendentals=0),
    )(*local)
    state, mixing, wind = map(near, local)
    shapes = [(halves, BEFORE[-1] * columns + TILE, LANES)] + [(halves, CORNER_SIZE + TILE, LANES)] * 2
    shapes += [(1, BEFORE[-1] * rows + TILE, LANES)] * halves
    to_x, to_1, to_2, *to_y = pl.pallas_call(
        pack_kernel, out_shape=[pltpu.VMEM(s, jnp.float32) for s in shapes],
        in_specs=[SMEM, SMEM, VMEM, VMEM, VMEM], out_specs=[VMEM] * len(shapes), compiler_params=small,
    )(where, code, state, other, mixing)
    halo_x = lax.ppermute(to_x, axes, partners(1, 0))
    halo_y = [lax.ppermute(y, axes, partners(0, 1)) for y in to_y]
    corner_1 = lax.ppermute(to_1, axes, partners(1, 1))
    corner_2 = lax.ppermute(to_2, axes, partners(1, -1))
    halo_x, halo_y, corner_1, corner_2 = lax.optimization_barrier((halo_x, halo_y, corner_1, corner_2))
    passed_y = [near(lax.ppermute(y, "tm", swap)) for y in halo_y]
    halo_x, corner_1, corner_2, *halo_y = map(near, (halo_x, corner_1, corner_2, *halo_y))
    half = rows // 2
    plane = (halves, half + 2 * HALO, columns + 2 * HALO + TILE, LANES)
    planes = [pltpu.VMEM(s, jnp.float32) for s in ((2, *plane), (2, *plane), plane, (2, *plane), (2, *plane), (2, *plane))]
    params = pltpu.CompilerParams(vmem_limit_bytes=LIMIT)
    filled = pl.pallas_call(
        fill_kernel, out_shape=planes, in_specs=[SMEM, SMEM] + [VMEM] * (7 + halves), out_specs=[VMEM] * 6,
        scratch_shapes=[pltpu.SMEM((3 * (half + 2 * HALO),), jnp.int32)], compiler_params=small,
        cost_estimate=pl.CostEstimate(flops=0, bytes_accessed=1 << 23, transcendentals=0),
    )(where, code, wind, state, other, mixing, halo_x, corner_1, corner_2, *halo_y)
    mine, theirs, *_ = pl.pallas_call(
        functools.partial(pair_kernel, halves), out_shape=[pltpu.VMEM((2, half, columns, levels), jnp.float32)] * 2 + planes,
        in_specs=[SMEM, SMEM] + [VMEM] * (10 + 2 * halves), out_specs=[VMEM] * 8,
        input_output_aliases={6 + 2 * halves + k: 2 + k for k in range(6)},
        scratch_shapes=[pltpu.VMEM((2, *plane), jnp.float32)] * 6 + [
            pltpu.VMEM((2, 2, half, columns, levels), jnp.float32), pltpu.SMEM((3 * (half + 2 * HALO),), jnp.int32)],
        compiler_params=params,
    )(where, code, wind, halo_x, corner_1, corner_2, *halo_y, *passed_y, *map(near, filled))
    got = lax.ppermute(theirs, "tm", swap)
    middle, final = pl.pallas_call(
        merge_kernel, out_shape=[of(*state.shape)] * 2, in_specs=[SMEM, VMEM, VMEM], out_specs=[ANY] * 2,
        scratch_shapes=[pltpu.SemaphoreType.DMA((4,))], compiler_params=small,
    )(where, near(mine), near(got))
    return middle[None], final[None]


def padded(x, sides, width):
    for axis, dim in sides:
        devices, length = lax.axis_size(axis), x.shape[dim]
        up = [(i, i + 1) for i in range(devices - 1)]
        down = [(j, i) for i, j in up]
        before = lax.ppermute(lax.slice_in_dim(x, length - width, length, axis=dim), axis, up)
        after = lax.ppermute(lax.slice_in_dim(x, 0, width, axis=dim), axis, down)
        x = jnp.concatenate([before, x, after], axis=dim)
    return x


def tendency(u, sign_x, sign_y, strength, wind, mixing):
    rows, columns = mixing.shape[:2]

    def beside(source, step_x, step_y):
        return source[2 + step_x:2 + step_x + rows, 2 + step_y:2 + step_y + columns]

    centre = beside(u, 0, 0)
    act = 0.5 * growth(u)
    spread = sum((beside(act, 0, 0) + beside(act, *s)) * (beside(u, *s) - centre) for s in ((1, 0), (-1, 0), (0, 1), (0, -1)))
    near_x, far_x = (jnp.where(sign_x > 0, beside(u, -k, 0), beside(u, k, 0)) for k in (1, 2))
    near_y, far_y = (jnp.where(sign_y > 0, beside(u, 0, -k), beside(u, 0, k)) for k in (1, 2))
    carried = wind[0] * (3.0 * centre - 4.0 * near_x + far_x) + wind[1] * (3.0 * centre - 4.0 * near_y + far_y)
    below = jnp.concatenate([centre[:, :, :1], centre[:, :, :-1]], axis=2)
    above = jnp.concatenate([centre[:, :, 1:], centre[:, :, -1:]], axis=2)
    return strength * spread - 0.5 * carried + mixing * (below + above - 2.0 * centre)


def slice_shards(state, code, wind, mixing, sizes):
    word = code[0, 0]
    strength = jnp.where(word // 4 == 1, diffusion_high, diffusion_low)

    def rate_of(u):
        return tendency(padded(u, (("gx", 0), ("gy", 1)), 2), 1 - 2 * (word % 2), 1 - 2 * (word // 2 % 2), strength, wind, mixing)

    start_rate = rate_of(state)
    last, rates = state, (start_rate,) * 3
    for _ in range(SWEEPS):
        arrived = lax.ppermute((last, rates[2]), "tm", [(i, i + 1) for i in range(sizes[0] - 1)])
        first, g0 = (jnp.where(lax.axis_index("tm") == 0, a, b) for a, b in zip((state, start_rate), arrived))
        middle = first + half_step * (g0 - rates[0]) + time_step * sum(w * r for w, r in zip(first_weights, rates))
        g1 = rate_of(middle)
        last = middle + half_step * (g1 - rates[1]) + time_step * sum(w * r for w, r in zip(second_weights, rates))
        rates = g0, g1, rate_of(last)
    return middle[None], last[None]


def solution(mesh):
    sizes = tuple(mesh.shape[a] for a in ("tm", "gx", "gy"))
    run = pair_shards if sizes[0] == 2 else slice_shards

    def shards(start_states, wind_code, wind_profile, vertical_mix):
        return run(start_states[0], wind_code, wind_profile, vertical_mix, sizes)

    in_specs = (P("tm", "gx", "gy", None), P("gx", "gy"), P(), P("gx", "gy", None))
    out_specs = (P("tm", "gx", "gy", None), P("tm", "gx", "gy", None))
    return jax.shard_map(shards, mesh=mesh, in_specs=in_specs, out_specs=out_specs, check_vma=False)
```

```python
import functools
import jax
import jax.numpy as jnp
from jax import lax
from jax.experimental import pallas as pl
from jax.experimental.pallas import tpu as pltpu
from jax.sharding import PartitionSpec as P

SWEEPS = 3
HALO = 4 * SWEEPS
LANES = 128
TILE = 8
time_step = 0.5
half_step = 0.25
diffusion_low = 0.04
diffusion_high = 0.1
first_weights = (5.0 / 24.0, 1.0 / 3.0, -1.0 / 24.0)
second_weights = (-1.0 / 24.0, 1.0 / 3.0, 5.0 / 24.0)


def row_classes(reach, own):
    steps = reach // 2
    groups = {}
    for a in range(steps + 1):
        beside = 2 * (steps - a) if a else reach
        groups.setdefault((-(-(own + 2 * beside) // TILE), a == 0), []).append((a, beside))
    out = []
    for (tiles, _), members in sorted(groups.items()):
        beside = max(b for _, b in members)
        begins = range(max(2, HALO + own + beside - TILE * tiles), HALO - beside + 1)
        cuts = lambda begin: sum(begin < e < begin + TILE * tiles and (e - begin) % TILE > 0 for e in (HALO, HALO + own))
        out.append((tiles, min(begins, key=cuts), members[0][0], members[-1][0]))
    return out


def growth(u):
    return 1.5 - 1.0 / (1.0 + u * u)


def sweeps(stages, part, own_rows, own_columns, codes, wind, mix, start, mid, last_1, last_2, f, g1, g1b, g2, g2b,
           act_a, act_b, write):
    halves = mix.shape[0]
    slices, parts = range(start.shape[0]), range(halves)
    scale = 0.5 * half_step
    lane = lax.broadcasted_iota(jnp.int32, (TILE, LANES), 1)
    line = lax.broadcasted_iota(jnp.int32, (TILE, LANES), 0)
    bottom, top = lane == 0, lane == LANES - 1
    cx = [jnp.broadcast_to(-0.5 * half_step * wind[0:1, z * LANES:(z + 1) * LANES], (TILE, LANES)) for z in parts]
    cy = [jnp.broadcast_to(-0.5 * half_step * wind[1:2, z * LANES:(z + 1) * LANES], (TILE, LANES)) for z in parts]
    c3 = [3.0 * (a + b) for a, b in zip(cx, cy)]

    def merge(edges, values):
        got = values[-1]
        for e, value in zip(reversed(edges), reversed(values[:-1])):
            got = jnp.where(line < e, value, got)
        return got

    def evaluate(reach, source, active, finish):
        def block(x, count, column, tiles):
            rows = range(count)
            puts, below_flux = [], {}
            for k in range(tiles):
                y = column + TILE * k
                edges = [e - y for e in (HALO, HALO + own_columns) if y < e < y + TILE]
                sides = [sum(p >= e for e in (HALO, HALO + own_columns)) for p in [y] + [y + e for e in edges]]
                words = [codes[x * 3 + j] for j in sides]
                kh = [jnp.where(w >= 8, 0.0, jnp.where(w >= 4, scale * diffusion_high, scale * diffusion_low)) for w in words]
                step_x = [1 - 2 * (w & 1) for w in words]
                step_y = [1 - (w & 2) for w in words]
                strength = merge(edges, [jnp.full((TILE, LANES), s, jnp.float32) for s in kh])
                rates = {}
                for n in slices:
                    def u_at(z, i, j):
                        return source[n, z, x + i, pl.ds(y + j, TILE), :]

                    def a_at(z, i, j):
                        return active[n, z, x + i, pl.ds(y + j, TILE), :]

                    centre = {(z, r): u_at(z, r, 0) for z in parts for r in rows}
                    ups = {c: pltpu.roll(u, LANES - 1, 1) for c, u in centre.items()}
                    downs = {c: pltpu.roll(u, 1, 1) for c, u in centre.items()}
                    total = {}
                    for z in parts:
                        col = [u_at(z, -1, 0)] + [centre[z, r] for r in rows] + [u_at(z, count, 0)]
                        act = [a_at(z, i, 0) for i in range(-1, count + 1)]
                        flux = [(act[i] + act[i + 1]) * (col[i + 1] - col[i]) for i in range(count + 1)]
                        for r in rows:
                            uc, ac = col[r + 1], act[r + 1]
                            up = (ac + a_at(z, r, 1)) * (u_at(z, r, 1) - uc)
                            moved = pltpu.roll(up, 1, 0)
                            if k:
                                down = jnp.where(line == 0, below_flux[n, z, r], moved)
                            else:
                                down = (ac + a_at(z, r, -1)) * (uc - u_at(z, r, -1))
                            below_flux[n, z, r] = moved
                            spread = (flux[r + 1] - flux[r]) + (up - down)
                            near_x = merge(edges, [u_at(z, r - s, 0) for s in step_x])
                            far_x = merge(edges, [u_at(z, r - 2 * s, 0) for s in step_x])
                            near_y = merge(edges, [u_at(z, r, -s) for s in step_y])
                            far_y = merge(edges, [u_at(z, r, -2 * s) for s in step_y])
                            total[z, r] = ((strength * spread + c3[z] * uc) + cx[z] * (far_x - 4.0 * near_x)
                                           + cy[z] * (far_y - 4.0 * near_y))
                    for r in rows:
                        for z in parts:
                            u = centre[z, r]
                            above = jnp.where(top, ups[z + 1, r] if z + 1 < halves else u, ups[z, r])
                            below = jnp.where(bottom, downs[z - 1, r] if z else u, downs[z, r])
                            bend = (above - u) + (below - u)
                            rate = total[z, r] + mix[z, x + r, pl.ds(y, TILE), :] * bend
                            rates[n, z, r] = rate

                            def get(ref, m=n):
                                return ref[m, z, x + r, pl.ds(y, TILE), :]

                            def put(ref, value):
                                puts.append((ref, (n, z, x + r, y), value))
                            finish(get, put, n, rates.get((n - 1, z, r), rate), u, rate)
            for ref, at, value in puts:
                write(ref, at, value)

        for tiles, column, near, far in row_classes(reach, own_columns):
            column, tiles = part(column, tiles)
            if near == 0:
                group = 4 if own_rows % 4 == 0 else 2

                @pl.loop(0, own_rows // group, unroll=2)
                def _(i, column=column, tiles=tiles, group=group):
                    block(HALO + group * i, group, column, tiles)
            else:
                span = 2 * (far - near + 1)
                group = 4 if span % 4 == 0 else 2
                width = span // group

                @pl.loop(0, 2 * width, unroll=2 if group == 2 else 1)
                def _(i, column=column, tiles=tiles, near=near, far=far, width=width, group=group):
                    low = HALO - 2 * far + group * i
                    high = HALO + own_rows + 2 * (near - 1) + group * (i - width)
                    block(jnp.where(i < width, low, high), group, column, tiles)

    w1 = [time_step / half_step * w for w in first_weights]
    w2 = [time_step / half_step * w for w in second_weights]
    assert abs(sum(w1) - 1) < 1e-12 and abs(sum(w2) - 1) < 1e-12

    def end_1(get, put, n, earlier, u, rate):
        m = get(start, max(n - 1, 0)) + ((earlier - rate) + rate)
        put(f, rate)
        put(mid, m)
        put(act_b, growth(m))

    def end_2(get, put, n, earlier, u, rate):
        first = get(f)
        last = u + ((rate - first) + first)
        put(g1, rate)
        put(last_1, last)
        put(act_a, growth(last))

    def end_3(get, put, n, earlier, u, rate):
        begin = get(last_1, n - 1) if n else get(start, 0)
        g0 = earlier if n else get(f, 0)
        m = begin + g0 + (w1[0] - 1.0) * get(f, max(n - 1, 0)) + w1[1] * get(g1) + w1[2] * rate
        put(g2, rate)
        put(mid, m)
        put(act_b, growth(m))

    def end_4(get, put, n, earlier, u, rate):
        last = u + rate + w2[0] * get(f, max(n - 1, 0)) + (w2[1] - 1.0) * get(g1) + w2[2] * get(g2)
        put(g1b, rate)
        put(last_2, last)
        put(act_a, growth(last))

    def end_5(get, put, n, earlier, u, rate):
        begin = get(last_2, n - 1) if n else get(start, 0)
        g0 = earlier if n else get(f, 0)
        before = get(g2, n - 1) if n else get(f, 0)
        m = begin + g0 + (w1[0] - 1.0) * before + w1[1] * get(g1b) + w1[2] * rate
        put(g2b, rate)
        put(mid, m)
        put(act_b, growth(m))

    def end_6(get, put, n, earlier, u, rate):
        before = get(g2, n - 1) if n else get(f, 0)
        put("middle", u)
        put("final", u + rate + w2[0] * before + (w2[1] - 1.0) * get(g1b) + w2[2] * get(g2b))

    every = ((10, start, act_a, end_1), (8, mid, act_b, end_2), (6, last_1, act_a, end_3),
             (4, mid, act_b, end_4), (2, last_2, act_a, end_5), (0, mid, act_b, end_6))
    for stage in stages:
        evaluate(*every[stage])


def whole(column, tiles):
    return column, tiles


def apart(low, own_columns, passed):
    def part(column, tiles):
        end = HALO + own_columns
        if low:
            free = sum(column + TILE * k + TILE + 2 <= end for k in range(tiles))
            return (column + TILE * free, tiles - free) if passed else (column, free)
        bound = sum(column + TILE * k - 2 < HALO for k in range(tiles))
        return (column, bound) if passed else (column + TILE * bound, tiles - bound)
    return part


def outside(word, low_x, low_y):
    return jnp.where(word == 0, 8 + (0 if low_x else 1) + (0 if low_y else 2), word - 1)


DEPTHS = (HALO, HALO, HALO - 2)


def corner_rows():
    out, offset = [], 0
    for a, depth in enumerate(DEPTHS):
        for d in range(depth - 2):
            wide = depth - 2 * (d // 2 + 1)
            out.append((a, d, offset, wide))
            offset += wide
    return out, offset


CORNER_ROWS, CORNER_SIZE = corner_rows()
BEFORE = tuple(sum(DEPTHS[:a]) for a in range(len(DEPTHS) + 1))


def load_kernel(*refs):
    made = [pltpu.make_async_copy(a, b, refs[6].at[k]) for k, (a, b) in enumerate(zip(refs[:3], refs[3:6]))]
    for one in made:
        one.start()
    for one in made:
        one.wait()


def pack_kernel(where_ref, code, own, other, mixing, beside_x, diagonal_1, diagonal_2, *beside_y):
    t = where_ref[0]
    rows, columns, levels = own.shape
    word = jnp.full((TILE, LANES), (code[0, 0] + 1).astype(jnp.float32))
    for ref in (beside_x, diagonal_1, diagonal_2, *beside_y):
        ref[0, pl.ds(ref.shape[1] - TILE, TILE), :] = word

    def side(low):
        arrays = (own, other, mixing) if low else (other, own, mixing)
        for z in range(levels // LANES):
            lanes = pl.ds(z * LANES, LANES)
            for a, depth in enumerate(DEPTHS):
                for i in range(depth):
                    x = i if low else rows - depth + i
                    beside_x[z, pl.ds((BEFORE[a] + i) * columns, columns), :] = arrays[a][x, :, lanes]
            for a, d, offset, wide in CORNER_ROWS:
                x = d if low else rows - 1 - d
                near, far = arrays[a][x, pl.ds(0, wide), lanes], arrays[a][x, pl.ds(columns - wide, wide), lanes]
                diagonal_1[z, pl.ds(offset, wide), :] = near if low else far
                diagonal_2[z, pl.ds(offset, wide), :] = far if low else near

        @pl.loop(0, rows // 2)
        def _(i):
            for x in (2 * i, 2 * i + 1):
                for z in range(levels // LANES):
                    for a, depth in enumerate(DEPTHS):
                        line = arrays[a][x, pl.ds(0 if low else columns - depth, depth), pl.ds(z * LANES, LANES)]
                        beside_y[z][0, pl.ds(BEFORE[a] * rows + x * depth, depth), :] = line

    pl.when(t == 0)(lambda: side(True))
    pl.when(t != 0)(lambda: side(False))


def filler(start, act, mix):
    def fill(a, z, x, y, value):
        at = (z, x, pl.ds(y, value.shape[0]), slice(None))
        if a < 2:
            start[(a, *at)] = value
            act[(a, *at)] = growth(value)
        else:
            mix[at] = half_step * value
    return fill


def fill_y(fill, arrived, low, beyond, own_shape):
    block_rows, columns, levels = own_shape
    inner = block_rows // 2 + HALO
    at_own, from_own = (HALO, 0) if low else (0, block_rows - inner)

    @pl.loop(0, inner // 4)
    def _(group):
        for r in range(4):
            i = 4 * group + r
            for z in range(levels // LANES):
                for a, depth in enumerate(DEPTHS):
                    value = arrived[z][0, pl.ds(BEFORE[a] * block_rows + (from_own + i) * depth, depth), :]
                    fill(a, z, at_own + i, HALO + columns if beyond else HALO - depth, value)


def fill_codes(low, code, words, codes, inner):
    word_x, word_y, word_p, word_1, word_2 = words
    at_own, at_x = (HALO, 0) if low else (0, inner)
    word_low, word_high = (word_y, word_p) if low else (word_p, word_y)
    corner_low, corner_high = (word_1, word_2) if low else (word_2, word_1)

    @pl.loop(0, inner)
    def _(i):
        codes[(at_own + i) * 3] = outside(word_low, True, True)
        codes[(at_own + i) * 3 + 1] = code[0, 0]
        codes[(at_own + i) * 3 + 2] = outside(word_high, True, False)

    @pl.loop(0, HALO)
    def _(i):
        codes[(at_x + i) * 3] = outside(corner_low, low, True)
        codes[(at_x + i) * 3 + 1] = outside(word_x, low, True)
        codes[(at_x + i) * 3 + 2] = outside(corner_high, low, False)


def word_of(ref):
    return jnp.max(ref[0, pl.ds(ref.shape[1] - TILE, TILE), :]).astype(jnp.int32)


def store(ref, at, value):
    n, z, x, y = at
    ref[n, z, x, pl.ds(y, TILE), :] = value


def fill_kernel(where_ref, code, wind, own, other, mixing, halo_x, corner_1, corner_2, *rest):
    t = where_ref[0]
    block_rows, columns, levels = own.shape
    halves = levels // LANES
    halo_y, (start, act_a, mix, f, mid, act_b, codes) = rest[:halves], rest[halves:]
    inner = block_rows // 2 + HALO
    fill = filler(start, act_a, mix)
    words = [word_of(halo_x), word_of(halo_y[0]), 0, word_of(corner_1), word_of(corner_2)]

    def side(low):
        at_own, from_own = (HALO, 0) if low else (0, block_rows - inner)
        low_corner, high_corner = (corner_1, corner_2) if low else (corner_2, corner_1)
        arrays = (own, other, mixing) if low else (other, own, mixing)
        fill_codes(low, code, words, codes, inner)

        @pl.loop(0, inner // 4)
        def _(group):
            for r in range(4):
                i = 4 * group + r
                for z in range(halves):
                    for a in range(len(DEPTHS)):
                        for y in range(0, columns, TILE):
                            fill(a, z, at_own + i, HALO + y, arrays[a][from_own + i, pl.ds(y, TILE), pl.ds(z * LANES, LANES)])

        fill_y(fill, halo_y, low, not low, own.shape)
        for z in range(halves):
            for a, depth in enumerate(DEPTHS):
                for i in range(depth):
                    x = HALO - depth + i if low else inner + i
                    for y in range(0, columns, TILE):
                        fill(a, z, x, HALO + y, halo_x[z, pl.ds((BEFORE[a] + i) * columns + y, TILE), :])
            for a, d, offset, wide in CORNER_ROWS:
                x = HALO - 1 - d if low else inner + d
                fill(a, z, x, HALO - wide, low_corner[z, pl.ds(offset, wide), :])
                fill(a, z, x, HALO + columns, high_corner[z, pl.ds(offset, wide), :])
        sweeps((0,), apart(low, columns, False), block_rows // 2, columns, codes, wind, mix, start, mid, None, None, f,
               None, None, None, None, act_a, act_b, store)

    pl.when(t == 0)(lambda: side(True))
    pl.when(t != 0)(lambda: side(False))


def pair_kernel(halves, where_ref, code, wind, halo_x, corner_1, corner_2, *rest):
    halo_y, passed_y = rest[:halves], rest[halves:2 * halves]
    mine, theirs, start, act_a, mix, f, mid, act_b, last_1, last_2, g1, g1b, g2, g2b, both, codes = rest[2 * halves + 6:]
    t = where_ref[0]
    half, columns = both.shape[2:4]
    words = [word_of(r) for r in (halo_x, halo_y[0], passed_y[0], corner_1, corner_2)]

    def run(stages, part, write):
        sweeps(stages, part, half, columns, codes, wind, mix, start, mid, last_1, last_2, f, g1, g1b, g2, g2b, act_a, act_b, write)

    def side(low):
        fill_codes(low, code, words, codes, half + HALO)
        fill_y(filler(start, act_a, mix), passed_y, low, low, (2 * half, columns, both.shape[4]))
        run((0,), apart(low, columns, True), store)

    pl.when(t == 0)(lambda: side(True))
    pl.when(t != 0)(lambda: side(False))

    def write(ref, at, value):
        n, z, x, y = at
        if isinstance(ref, str):
            place = jnp.where(t == n, 0, 1)
            both[place, 0 if ref == "middle" else 1, x - HALO, pl.ds(y - HALO, TILE), pl.ds(z * LANES, LANES)] = value
        else:
            store(ref, at, value)

    run(range(1, 6), whole, write)
    mine[...] = both[0]
    theirs[...] = both[1]


def place_kernel(where_ref, part, *rest):
    middle, final, semaphores = rest[-3:]
    own = len(rest) == 3
    half = part.shape[1]

    def place(begin):
        made = [pltpu.make_async_copy(part.at[k], out.at[pl.ds(begin, half)], semaphores.at[k]) for k, out in enumerate((middle, final))]
        for one in made:
            one.start()
        for one in made:
            one.wait()

    pl.when(where_ref[0] == 0)(lambda: place(0 if own else half))
    pl.when(where_ref[0] != 0)(lambda: place(half if own else 0))


VMEM = pl.BlockSpec(memory_space=pltpu.VMEM)
SMEM = pl.BlockSpec(memory_space=pltpu.SMEM)
ANY = pl.BlockSpec(memory_space=pl.ANY)
LIMIT = 30 * 2**20


def of(*shape):
    return jax.ShapeDtypeStruct(shape, jnp.float32)


def near(x):
    return pltpu.with_memory_space_constraint(x, pltpu.VMEM)


def pair_shards(state, code, wind, mixing, sizes):
    axes = ("tm", "gx", "gy")
    rows, columns, levels = state.shape
    halves = levels // LANES
    t = lax.axis_index("tm")
    where = t.astype(jnp.int32).reshape(1)

    def partners(step_x, step_y):
        pairs = []
        for x in range(sizes[1]):
            for y in range(sizes[2]):
                u, v = x - step_x, y - step_y
                if 0 <= u < sizes[1] and 0 <= v < sizes[2]:
                    here, there = x * sizes[2] + y, (sizes[1] + u) * sizes[2] + v
                    pairs += [(here, there), (there, here)]
        return pairs

    swap = [(0, 1), (1, 0)]
    small = pltpu.CompilerParams(vmem_limit_bytes=4 * 2**20)
    other = near(lax.ppermute(state, "tm", swap))
    local = state, mixing, wind
    local = pl.pallas_call(
        load_kernel, out_shape=[pltpu.VMEM(x.shape, jnp.float32) for x in local],
        in_specs=[ANY] * 3, out_specs=[VMEM] * 3, scratch_shapes=[pltpu.SemaphoreType.DMA((3,))],
        compiler_params=pltpu.CompilerParams(vmem_limit_bytes=60 * 2**20),
        cost_estimate=pl.CostEstimate(flops=0, bytes_accessed=16 * state.size, transcendentals=0),
    )(*local)
    state, mixing, wind = map(near, local)
    shapes = [(halves, BEFORE[-1] * columns + TILE, LANES)] + [(halves, CORNER_SIZE + TILE, LANES)] * 2
    shapes += [(1, BEFORE[-1] * rows + TILE, LANES)] * halves
    to_x, to_1, to_2, *to_y = pl.pallas_call(
        pack_kernel, out_shape=[pltpu.VMEM(s, jnp.float32) for s in shapes],
        in_specs=[SMEM, SMEM, VMEM, VMEM, VMEM], out_specs=[VMEM] * len(shapes), compiler_params=small,
    )(where, code, state, other, mixing)
    halo_x = lax.ppermute(to_x, axes, partners(1, 0))
    halo_y = [lax.ppermute(y, axes, partners(0, 1)) for y in to_y]
    corner_1 = lax.ppermute(to_1, axes, partners(1, 1))
    corner_2 = lax.ppermute(to_2, axes, partners(1, -1))
    halo_x, halo_y, corner_1, corner_2 = lax.optimization_barrier((halo_x, halo_y, corner_1, corner_2))
    passed_y = [near(lax.ppermute(y, "tm", swap)) for y in halo_y]
    halo_x, corner_1, corner_2, *halo_y = map(near, (halo_x, corner_1, corner_2, *halo_y))
    half = rows // 2
    plane = (halves, half + 2 * HALO, columns + 2 * HALO + TILE, LANES)
    planes = [pltpu.VMEM(s, jnp.float32) for s in ((2, *plane), (2, *plane), plane, (2, *plane), (2, *plane), (2, *plane))]
    params = pltpu.CompilerParams(vmem_limit_bytes=LIMIT)
    filled = pl.pallas_call(
        fill_kernel, out_shape=planes, in_specs=[SMEM, SMEM] + [VMEM] * (7 + halves), out_specs=[VMEM] * 6,
        scratch_shapes=[pltpu.SMEM((3 * (half + 2 * HALO),), jnp.int32)], compiler_params=small,
        cost_estimate=pl.CostEstimate(flops=0, bytes_accessed=1 << 23, transcendentals=0),
    )(where, code, wind, state, other, mixing, halo_x, corner_1, corner_2, *halo_y)
    mine, theirs, *_ = pl.pallas_call(
        functools.partial(pair_kernel, halves), out_shape=[pltpu.VMEM((2, half, columns, levels), jnp.float32)] * 2 + planes,
        in_specs=[SMEM, SMEM] + [VMEM] * (10 + 2 * halves), out_specs=[VMEM] * 8,
        input_output_aliases={6 + 2 * halves + k: 2 + k for k in range(6)},
        scratch_shapes=[pltpu.VMEM((2, *plane), jnp.float32)] * 6 + [
            pltpu.VMEM((2, 2, half, columns, levels), jnp.float32), pltpu.SMEM((3 * (half + 2 * HALO),), jnp.int32)],
        compiler_params=params,
    )(where, code, wind, halo_x, corner_1, corner_2, *halo_y, *passed_y, *map(near, filled))
    got = lax.ppermute(theirs, "tm", swap)
    outs = [of(*state.shape)] * 2
    halves_done = pl.pallas_call(
        place_kernel, out_shape=outs, in_specs=[SMEM, VMEM], out_specs=[ANY] * 2,
        scratch_shapes=[pltpu.SemaphoreType.DMA((2,))], compiler_params=small,
        cost_estimate=pl.CostEstimate(flops=0, bytes_accessed=1 << 22, transcendentals=0),
    )(where, near(mine))
    middle, final = pl.pallas_call(
        place_kernel, out_shape=outs, in_specs=[SMEM, VMEM, ANY, ANY], out_specs=[ANY] * 2,
        input_output_aliases={2: 0, 3: 1}, scratch_shapes=[pltpu.SemaphoreType.DMA((2,))], compiler_params=small,
    )(where, near(got), *halves_done)
    return middle[None], final[None]


def padded(x, sides, width):
    for axis, dim in sides:
        devices, length = lax.axis_size(axis), x.shape[dim]
        up = [(i, i + 1) for i in range(devices - 1)]
        down = [(j, i) for i, j in up]
        before = lax.ppermute(lax.slice_in_dim(x, length - width, length, axis=dim), axis, up)
        after = lax.ppermute(lax.slice_in_dim(x, 0, width, axis=dim), axis, down)
        x = jnp.concatenate([before, x, after], axis=dim)
    return x


def tendency(u, sign_x, sign_y, strength, wind, mixing):
    rows, columns = mixing.shape[:2]

    def beside(source, step_x, step_y):
        return source[2 + step_x:2 + step_x + rows, 2 + step_y:2 + step_y + columns]

    centre = beside(u, 0, 0)
    act = 0.5 * growth(u)
    spread = sum((beside(act, 0, 0) + beside(act, *s)) * (beside(u, *s) - centre) for s in ((1, 0), (-1, 0), (0, 1), (0, -1)))
    near_x, far_x = (jnp.where(sign_x > 0, beside(u, -k, 0), beside(u, k, 0)) for k in (1, 2))
    near_y, far_y = (jnp.where(sign_y > 0, beside(u, 0, -k), beside(u, 0, k)) for k in (1, 2))
    carried = wind[0] * (3.0 * centre - 4.0 * near_x + far_x) + wind[1] * (3.0 * centre - 4.0 * near_y + far_y)
    below = jnp.concatenate([centre[:, :, :1], centre[:, :, :-1]], axis=2)
    above = jnp.concatenate([centre[:, :, 1:], centre[:, :, -1:]], axis=2)
    return strength * spread - 0.5 * carried + mixing * (below + above - 2.0 * centre)


def slice_shards(state, code, wind, mixing, sizes):
    word = code[0, 0]
    strength = jnp.where(word // 4 == 1, diffusion_high, diffusion_low)

    def rate_of(u):
        return tendency(padded(u, (("gx", 0), ("gy", 1)), 2), 1 - 2 * (word % 2), 1 - 2 * (word // 2 % 2), strength, wind, mixing)

    start_rate = rate_of(state)
    last, rates = state, (start_rate,) * 3
    for _ in range(SWEEPS):
        arrived = lax.ppermute((last, rates[2]), "tm", [(i, i + 1) for i in range(sizes[0] - 1)])
        first, g0 = (jnp.where(lax.axis_index("tm") == 0, a, b) for a, b in zip((state, start_rate), arrived))
        middle = first + half_step * (g0 - rates[0]) + time_step * sum(w * r for w, r in zip(first_weights, rates))
        g1 = rate_of(middle)
        last = middle + half_step * (g1 - rates[1]) + time_step * sum(w * r for w, r in zip(second_weights, rates))
        rates = g0, g1, rate_of(last)
    return middle[None], last[None]


def solution(mesh):
    sizes = tuple(mesh.shape[a] for a in ("tm", "gx", "gy"))
    run = pair_shards if sizes[0] == 2 else slice_shards

    def shards(start_states, wind_code, wind_profile, vertical_mix):
        return run(start_states[0], wind_code, wind_profile, vertical_mix, sizes)

    in_specs = (P("tm", "gx", "gy", None), P("gx", "gy"), P(), P("gx", "gy", None))
    out_specs = (P("tm", "gx", "gy", None), P("tm", "gx", "gy", None))
    return jax.shard_map(shards, mesh=mesh, in_specs=in_specs, out_specs=out_specs, check_vma=False)
```
